256 devices in a mesh: row: 8 (over z_lo, y), col: 32 (over z_hi, x, core).
Axes of the slice: x: 4, y: 4, z: 8 (z_hi: 4, z_lo: 2; z = z_hi * 2 + z_lo), core: 2. Of those that a mesh axis runs over, the one named last changes fastest.
Arguments:
- matrix: float32 [8, 8, 256, 2, 32, 256], P(None, 'row', None, None, 'col'), as said below
Outputs:
- factored: float32 [8, 8, 256, 2, 32, 256], P(None, 'row', None, None, 'col')
Inputs may be any that keep to these rules, and one draw needn't show every extreme that they name: `matrix`: symmetric positive definite.
All inputs are finite; a program needn't handle non-finite values.
Results may differ from the reference program's by a relative error of at most 0.00017.
Values sent between devices are 32-bit elements; how exact they have to be, the bound alone decides.
A program may use at most 64 MiB of HBM per device.

```python
import jax
import jax.numpy as jnp
from jax import lax

M = 16384
NB = 256
GRID_ROWS = 8
GRID_COLS = 32
ROW_SLOTS = 8
COL_SLOTS = 2


def draw_matrix(key, part):
    key = jax.random.fold_in(key, 17)
    key_factor, key_noise, key_diagonal = jax.random.split(key, 3)
    factor_width = 2 * NB
    factor = jax.random.normal(key_factor, (M, factor_width), jnp.float32)
    raw_noise = jax.random.normal(key_noise, (M, M), jnp.float32)
    diagonal = jax.random.uniform(key_diagonal, (M,), jnp.float32, 2.0, 4.0)
    factor = factor * factor_width ** (-0.25)
    product = jnp.dot(factor, factor.T, precision=lax.Precision.HIGHEST, preferred_element_type=jnp.float32)
    symmetric_noise = (raw_noise + raw_noise.T) * (0.5 / (2.0 * M) ** 0.5)
    dense = product + symmetric_noise + jnp.diag(diagonal)
    return dense.reshape(ROW_SLOTS, GRID_ROWS, NB, COL_SLOTS, GRID_COLS, NB)


def setup_inputs(seed: int = 0) -> dict:
    splits = jax.random.split(jax.random.key(seed), 2)
    matrix = draw_matrix(jax.random.fold_in(splits[1], 71), 0)
    return dict(matrix=matrix)


def reference(matrix):
    dense = matrix.reshape(M, M)
    for step_index in range(2):
        begin_at = step_index * NB
        end_at = begin_at + NB
        factor = jnp.linalg.cholesky(dense[begin_at:end_at, begin_at:end_at])
        below_rows = dense[end_at:, begin_at:end_at]
        panel_rows = jax.scipy.linalg.solve_triangular(factor, below_rows.T, lower=True).T
        trailing = dense[end_at:, end_at:] - jnp.dot(panel_rows.astype(jnp.float32), panel_rows.T.astype(jnp.float32), precision=lax.Precision.HIGHEST, preferred_element_type=jnp.float32)
        dense = dense.at[end_at:, end_at:].set(trailing)
        dense = dense.at[begin_at:end_at, begin_at:end_at].set(factor)
        dense = dense.at[end_at:, begin_at:end_at].set(panel_rows)
        dense = dense.at[begin_at:end_at, end_at:].set(jnp.zeros((NB, M - end_at), jnp.float32))
    return dense.reshape(matrix.shape)
```

```python
import functools

import jax
import jax.numpy as jnp
from jax import lax
from jax.experimental import pallas as pl
from jax.experimental.pallas import tpu as pltpu
from jax.sharding import PartitionSpec as P

F32 = jnp.float32
BF16 = jnp.bfloat16
MESH = pl.DeviceIdType.MESH
HIGHEST = lax.Precision.HIGHEST
NB = 256
LEAF = 128
CHUNKS = [(i, j) for i in range(4) for j in range(i + 1)]


def leaf_inverse(block):
    n = block.shape[0]
    sub = lax.broadcasted_iota(jnp.int32, (8, n), 0)
    lane = lax.broadcasted_iota(jnp.int32, (8, n), 1)
    rows = [block[8 * g : 8 * g + 8] for g in range(n // 8)]
    inv = [jnp.where(lane == sub + 8 * g, 1.0, 0.0).astype(F32) for g in range(n // 8)]
    out = []
    for t in range(n // 8):
        cols = [[jnp.broadcast_to(r[:, 8 * t + j : 8 * t + j + 1], (8, n)) for r in rows] for j in range(8)]
        for j in range(8):
            r = lax.rsqrt(jnp.broadcast_to(cols[j][0][j : j + 1], (8, n)))
            lcol = [c * r for c in cols[j]]
            lead = lcol[0]
            for k in range(j + 1, 8):
                f = jnp.broadcast_to(lead[k : k + 1], (8, n))
                cols[k] = [c - l * f for c, l in zip(cols[k], lcol)]
            row = jnp.broadcast_to(rows[0][j : j + 1], (8, n)) * r
            irow = jnp.broadcast_to(inv[0][j : j + 1], (8, n)) * r
            low = jnp.where(sub > j, lead, 0.0)
            rows = [rows[0] - low * row] + [a - l * row for a, l in zip(rows[1:], lcol[1:])]
            inv = [jnp.where(sub == j, irow, inv[0] - low * irow)] + [a - l * irow for a, l in zip(inv[1:], lcol[1:])]
        out.append(inv[0])
        rows, inv = rows[1:], inv[1:]
    return jnp.concatenate(out, 0)


def dot_full(a, b, trans_a=False):
    return lax.dot_general(
        a, b, (((0 if trans_a else 1,), (0,)), ((), ())), precision=HIGHEST, preferred_element_type=F32
    )


def factor_block(i, nb, d_ref, li_ref):
    n = LEAF
    s = slice(i * n, (i + 1) * n)
    m = leaf_inverse(d_ref[s, s])
    li_ref[s, s] = m
    if i:
        li_ref[s, : i * n] = -dot_full(m, d_ref[s, : i * n])
    if i + 1 < nb:
        r = dot_full(m, d_ref[s, (i + 1) * n :])
        for j in range(i + 1, nb):
            off = (j - i - 1) * n
            t = slice(j * n, (j + 1) * n)
            rj = r[:, off : off + n]
            d_ref[t, j * n :] = d_ref[t, j * n :] - dot_full(rj, r[:, off:], True)
            p = dot_full(rj, li_ref[s, : (i + 1) * n], True)
            if i:
                d_ref[t, : i * n] = d_ref[t, : i * n] + p[:, : i * n]
            d_ref[t, s] = p[:, i * n :]


def gather_kernel(x_ref, ar_ref, ac_ref, lo_ref, xin, xb, xt, d, li,
                  in_sem, loc_sem, sc_s, sc_r, zb_s, zb_r, xc_s, xc_r, cd_s, cd_r,
                  lc_s, lc_r, dg_s, dg_r, li_s, li_r):
    row = lax.axis_index("row")
    col = lax.axis_index("col")
    zl, y = row // 4, row % 4
    zh, x, co = col // 8, (col // 2) % 4, col % 2

    def dev(zl=zl, y=y, zh=zh, x=x, co=co):
        return (zl * 4 + y, (zh * 4 + x) * 2 + co)

    def rc(src, dst, ss, rs, to):
        return pltpu.make_async_remote_copy(
            src_ref=src, dst_ref=dst, send_sem=ss, recv_sem=rs, device_id=to, device_id_type=MESH
        )

    def piece(p, xq, zq):
        at = pl.multiple_of((4 * (xq // 2) + zq) * NB + (xq % 2) * LEAF, LEAF)
        return ar_ref.at[p, pl.ds(at, LEAF), :]

    top = row < 2
    root = (row == 0) & (col == 0)
    self_scatter = (row == co) & (x == 0)
    here = dev()

    is_z = (row == 0) & (col == 0)
    is_x = (row == 0) & (x == 0) & (co == 0)
    is_y = (row == 0) & (co == 0)
    is_l = (zl == 0) & (co == 0)
    is_c = co == 0

    load = pltpu.make_async_copy(x_ref.at[pl.ds(0, 4 * NB)], xin, in_sem)

    @pl.when(top)
    def _():
        load.start()

    bar = pltpu.get_barrier_semaphore()

    def greet(to):
        pl.semaphore_signal(bar, inc=1, device_id=to, device_id_type=MESH)

    one = lambda c: jnp.where(c, 1, 0)

    @pl.when(jnp.logical_not(self_scatter))
    def _():
        greet((co, zh * 8 + row))

    for k in range(1, 4):
        greet(dev(zh=(zh + k) % 4))
        greet(dev(x=(x + k) % 4))
    greet(dev(co=1 - co))
    edges = 7 + jnp.where(top, 4 - one(col % 8 == row), 0)
    for p in range(2):
        near, far, mid = (1, 2, 3) if p == 0 else (0, 3, 2)

        @pl.when((row == p + 4))
        def _():
            greet(dev(zl=0))

        @pl.when((y == near) | (y == mid))
        def _():
            greet(dev(y=p))

        @pl.when(y == far)
        def _():
            greet(dev(y=mid))

        edges = edges + 2 * one(y == p) + one(row == p) + one(y == mid)

    @pl.when(root)
    def _():
        greet((0, 1))
        greet((1, 1))

    edges = edges + one((row < 2) & (col == 1))

    @pl.when(jnp.logical_not(is_c))
    def _():
        greet(dev(co=0))

    @pl.when(is_c & jnp.logical_not(is_l))
    def _():
        greet(dev(zl=0))

    @pl.when(is_l & jnp.logical_not(is_y))
    def _():
        greet(dev(y=0))

    @pl.when(is_y & jnp.logical_not(is_x))
    def _():
        greet(dev(x=0))

    @pl.when(is_x & jnp.logical_not(is_z))
    def _():
        greet(dev(zh=0))

    edges = edges + 3 * one(is_z) + 3 * one(is_x) + 3 * one(is_y) + one(is_l) + one(is_c)
    pl.semaphore_wait(bar, edges)


    def scatter(q):
        return rc(xt.at[pl.ds(q * LEAF, LEAF)],
                  ar_ref.at[row, pl.ds(pl.multiple_of((4 * (q // 2) + zh) * NB + (q % 2) * LEAF, LEAF), LEAF), :],
                  sc_s.at[q], sc_r.at[0], (col % 8, (zh * 4 + q) * 2 + row))

    def scatter_in():
        return rc(piece(co, x, zh), piece(co, x, zh), sc_s.at[0], sc_r.at[0], dev(co=1 - co))

    def scatter_self():
        return pltpu.make_async_copy(xt.at[pl.ds(0, LEAF)], piece(co, x, zh), loc_sem.at[0])

    def z_out(k):
        return rc(piece(co, x, zh), piece(co, x, zh), zb_s.at[k - 1], zb_r.at[k - 1], dev(zh=(zh + k) % 4))

    def z_in(k):
        q = piece(co, x, (zh + 4 - k) % 4)
        return rc(q, q, zb_s.at[k - 1], zb_r.at[k - 1], dev(co=1 - co))

    def x_out(kz, kx):
        q = piece(co, x, (zh + 4 - kz) % 4)
        return rc(q, q, xc_s.at[kz, kx - 1], xc_r.at[kz, kx - 1], dev(x=(x + kx) % 4))

    def x_in(kz, kx):
        q = piece(co, (x + 4 - kx) % 4, (zh + 4 - kz) % 4)
        return rc(q, q, xc_s.at[kz, kx - 1], xc_r.at[kz, kx - 1], dev(co=1 - co))

    def c_out(kz, kx):
        q = piece(co, (x + 4 - kx) % 4, (zh + 4 - kz) % 4)
        return rc(q, q, cd_s.at[kz, kx], cd_r.at[kz, kx], dev(co=1 - co))

    def c_in(kz, kx):
        q = piece(1 - co, (x + 4 - kx) % 4, (zh + 4 - kz) % 4)
        return rc(q, q, cd_s.at[kz, kx], cd_r.at[kz, kx], dev(co=1 - co))

    def lc_part(p, h):
        return ac_ref.at[pl.ds(p * NB + h * LEAF, LEAF)]

    def lc_first(p, h, k):
        to = (dev(zl=1), dev(y=(p + 1) % 4), dev(y=(p + 3) % 4))[k]
        return rc(xb.at[pl.ds(h * LEAF, LEAF)], lc_part(p, h), lc_s.at[p, h, k], lc_r.at[p, h], to)

    def lc_next(p, h, k, to):
        return rc(lc_part(p, h), lc_part(p, h), lc_s.at[p, h, k], lc_r.at[p, h], to)

    def lc_in(p, h):
        return rc(lc_part(p, h), lc_part(p, h), lc_s.at[p, h, 0], lc_r.at[p, h], dev(co=1 - co))

    def diag_out(p):
        return rc(xb.at[:, pl.ds(0, NB)], d.at[pl.ds(p * NB, NB), pl.ds(NB, NB)], dg_s.at[0], dg_r.at[p], (0, 0))

    def diag_in(p):
        q = d.at[pl.ds(p * NB, NB), pl.ds(NB, NB)]
        return rc(q, q, dg_s.at[0], dg_r.at[p], (0, 1))

    def li_part(ref, c):
        i, j = CHUNKS[c]
        return ref.at[pl.ds(i * LEAF, LEAF), pl.ds(j * LEAF, LEAF)]

    def li_out(c, ref, k, to):
        return rc(li_part(ref, c), li_part(lo_ref, c), li_s.at[c, k], li_r.at[c], to)

    def li_in(c):
        q = li_part(lo_ref, c)
        return rc(q, q, li_s.at[c, 0], li_r.at[c], dev(co=1 - co))

    def li_edges(c, ref, what):
        def run(role, k, to):
            @pl.when(role)
            def _():
                cp = li_out(c, ref, k, to)
                cp.start() if what == "start" else cp.wait_send()

        for k in range(3):
            run(is_z, k, dev(zh=(zh + k + 1) % 4))
        for k in range(3):
            run(is_x, 3 + k, dev(x=(x + k + 1) % 4))
        for k in range(3):
            run(is_y, 6 + k, dev(y=(y + k + 1) % 4))
        run(is_l, 9, dev(zl=1))
        run(is_c, 10, dev(co=1))

    def li_pass(chunks):
        @pl.when(jnp.logical_not(root))
        def _():
            for c in chunks:
                li_in(c).wait_recv()
                li_edges(c, lo_ref, "start")

    def li_root(i):
        @pl.when(root)
        def _():
            if i == 0:
                d[pl.ds(0, NB), pl.ds(0, NB)] = xb[:, pl.ds(0, NB)]
                for p in range(2):
                    diag_in(p).wait_recv()
            factor_block(i, 4, d, li)
            for c, (a, _b) in enumerate(CHUNKS):
                if a == i:
                    li_edges(c, li, "start")
                    pltpu.make_async_copy(li_part(li, c), li_part(lo_ref, c), loc_sem.at[4 + c]).start()


    for p in range(2):

        @pl.when(row == p)
        def _():
            load.wait()
            for q in range(4):
                xb[:, pl.ds(q * LEAF, LEAF)] = xin[pl.ds(q, NB, stride=4), :]

            @pl.when(col == 1)
            def _():
                diag_out(p).start()

            for k in range(3):
                lc_first(p, 0, k).start()
            for q in range(4):
                xt[pl.ds(q * LEAF, LEAF), :] = xb[:, pl.ds(q * LEAF, LEAF)].T
            for q in range(1, 4):
                scatter(q).start()

            @pl.when(col % 8 == row)
            def _():
                scatter_self().start()

            @pl.when(col % 8 != row)
            def _():
                scatter(0).start()

            for k in range(3):
                lc_first(p, 1, k).start()
            pltpu.make_async_copy(xb, ac_ref.at[pl.ds(p * NB, NB)], loc_sem.at[1]).start()

    li_root(0)


    @pl.when(self_scatter)
    def _():
        scatter_self().wait()

    @pl.when(jnp.logical_not(self_scatter))
    def _():
        scatter_in().wait_recv()

    for k in range(1, 4):
        z_out(k).start()
        x_out(0, k).start()
    c_out(0, 0).start()

    li_root(1)

    for h in range(2):
        for p in range(2):
            near, far, mid = (1, 2, 3) if p == 0 else (0, 3, 2)

            @pl.when(row == p + 4)
            def _():
                lc_in(p, h).wait_recv()
                lc_next(p, h, 1, dev(y=(p + 1) % 4)).start()
                lc_next(p, h, 2, dev(y=(p + 3) % 4)).start()

            @pl.when(y == mid)
            def _():
                lc_in(p, h).wait_recv()
                lc_next(p, h, 0, dev(y=far)).start()

    li_root(2)

    for kz in range(1, 4):
        z_in(kz).wait_recv()
        for kx in range(1, 4):
            x_out(kz, kx).start()
        c_out(kz, 0).start()

    li_root(3)

    parts = [[0, 1, 2], [3, 4, 5], [], [6, 7, 8, 9]]
    for kz in range(4):
        for kx in range(1, 4):
            x_in(kz, kx).wait_recv()
            c_out(kz, kx).start()
        li_pass(parts[kz])

    for h in range(2):
        for p in range(2):
            near, far, mid = (1, 2, 3) if p == 0 else (0, 3, 2)

            @pl.when((y == near) | (y == far))
            def _():
                lc_in(p, h).wait_recv()

    for kz in range(4):
        for kx in range(4):
            c_in(kz, kx).wait_recv()
            c_out(kz, kx).wait_send()
            if kx:
                x_out(kz, kx).wait_send()
        if kz:
            z_out(kz).wait_send()

    for p in range(2):

        @pl.when(row == p)
        def _():
            @pl.when(col == 1)
            def _():
                diag_out(p).wait_send()

            for h in range(2):
                for k in range(3):
                    lc_first(p, h, k).wait_send()
            for q in range(1, 4):
                scatter(q).wait_send()

            @pl.when(col % 8 != row)
            def _():
                scatter(0).wait_send()

            pltpu.make_async_copy(xb, ac_ref.at[pl.ds(p * NB, NB)], loc_sem.at[1]).wait()

        near, far, mid = (1, 2, 3) if p == 0 else (0, 3, 2)
        for h in range(2):

            @pl.when(row == p + 4)
            def _():
                lc_next(p, h, 1, dev(y=(p + 1) % 4)).wait_send()
                lc_next(p, h, 2, dev(y=(p + 3) % 4)).wait_send()

            @pl.when(y == mid)
            def _():
                lc_next(p, h, 0, dev(y=far)).wait_send()

    for c in range(len(CHUNKS)):
        li_edges(c, lo_ref, "wait")

        @pl.when(root)
        def _():
            pltpu.make_async_copy(li_part(li, c), li_part(lo_ref, c), loc_sem.at[4 + c]).wait()


def gather(flat):
    any_spec = pl.BlockSpec(memory_space=pl.ANY)
    dma = pltpu.SemaphoreType.DMA
    return pl.pallas_call(
        gather_kernel,
        out_shape=[
            jax.ShapeDtypeStruct((2, 2048, NB), F32),
            jax.ShapeDtypeStruct((2 * NB, 2 * NB), F32),
            jax.ShapeDtypeStruct((2 * NB, 2 * NB), F32),
        ],
        in_specs=[any_spec],
        out_specs=[any_spec] * 3,
        scratch_shapes=[
            pltpu.VMEM((4 * NB, 128), F32),
            pltpu.VMEM((NB, 2 * NB), F32),
            pltpu.VMEM((2 * NB, NB), F32),
            pltpu.VMEM((2 * NB, 2 * NB), F32),
            pltpu.VMEM((2 * NB, 2 * NB), F32),
            dma, dma((14,)),
            dma((4,)), dma((1,)),
            dma((3,)), dma((3,)),
            dma((4, 3)), dma((4, 3)),
            dma((4, 4)), dma((4, 4)),
            dma((2, 2, 3)), dma((2, 2)),
            dma((1,)), dma((2,)),
            dma((10, 11)), dma((10,)),
        ],
        compiler_params=pltpu.CompilerParams(collective_id=0, has_side_effects=True, vmem_limit_bytes=32 << 20),
        name="gather_panel",
    )(flat)


def halves(a):
    hi = a.astype(BF16)
    return hi, (a - hi.astype(F32)).astype(BF16)


def dot3(a, b, trans_b=False):
    dims = (((1,), (1 if trans_b else 0,)), ((), ()))
    mm = lambda u, v: lax.dot_general(u, v, dims, preferred_element_type=F32)
    return mm(a[0], b[0]) + (mm(a[0], b[1]) + mm(a[1], b[0]))


def update_kernel(x_ref, ar_ref, ac_ref, li_ref, o_ref, u_hi, u_lo, l_hi, l_lo):
    slot = pl.program_id(0)
    row = lax.axis_index("row")
    col = lax.axis_index("col")

    @pl.when(slot == 0)
    def _():
        for i in range(4):
            for j in range(4):
                at = (pl.ds(i * LEAF, LEAF), pl.ds(j * LEAF, LEAF))
                if j > i:
                    l_hi[at] = jnp.zeros((LEAF, LEAF), BF16)
                    l_lo[at] = jnp.zeros((LEAF, LEAF), BF16)
                else:
                    v = li_ref[at]
                    if i == j:
                        r = lax.broadcasted_iota(jnp.int32, v.shape, 0)
                        c = lax.broadcasted_iota(jnp.int32, v.shape, 1)
                        v = jnp.where(c <= r, v, 0.0)
                    l_hi[at], l_lo[at] = halves(v)
        u = dot3((l_hi[...], l_lo[...]), halves(ac_ref[...]))
        u_hi[...], u_lo[...] = halves(u)

    a0 = halves(ar_ref[0])
    a1 = halves(ar_ref[1])
    top, low = pl.ds(0, NB), pl.ds(NB, NB)
    p0 = dot3(a0, (l_hi[top, top], l_lo[top, top]), True)
    p1 = dot3(a0, (l_hi[low, top], l_lo[low, top]), True) + dot3(a1, (l_hi[low, low], l_lo[low, low]), True)
    h0, h1 = halves(p0), halves(p1)
    upd = dot3(h0, (u_hi[top, :], u_lo[top, :])) + dot3(h1, (u_hi[low, :], u_lo[low, :]))
    grow = slot * 8 + row
    keep = grow >= 2
    for q in range(4):
        cols = slice(q * LEAF, (q + 1) * LEAF)
        v = jnp.where(keep, x_ref[0, pl.ds(q, NB, stride=4), :] - upd[:, cols], 0.0)
        o_ref[0, pl.ds(q, NB, stride=4), :] = v

    def put(p, mask):
        for q in range(2):
            v = p[:, q * LEAF : (q + 1) * LEAF]
            r = lax.broadcasted_iota(jnp.int32, v.shape, 0)
            c = lax.broadcasted_iota(jnp.int32, v.shape, 1) + q * LEAF
            o_ref[0, pl.ds(q, NB, stride=4), :] = jnp.where((c <= r) | jnp.logical_not(mask), v, 0.0)

    @pl.when(col == 0)
    def _():
        put(p0, grow == 0)

    @pl.when((col == 1) & (grow >= 1))
    def _():
        put(p1, grow == 1)


def update(flat, ar, ac, li):
    whole = pl.BlockSpec((2 * NB, 2 * NB), lambda s: (0, 0))
    slab = pl.BlockSpec((1, 4 * NB, 128), lambda s: (s, 0, 0))
    return pl.pallas_call(
        update_kernel,
        grid=(8,),
        out_shape=jax.ShapeDtypeStruct(flat.shape, F32),
        in_specs=[slab, pl.BlockSpec((2, NB, NB), lambda s: (0, s, 0)), whole, whole],
        out_specs=slab,
        scratch_shapes=[pltpu.VMEM((2 * NB, 2 * NB), BF16)] * 4,
        compiler_params=pltpu.CompilerParams(vmem_limit_bytes=32 << 20),
        name="update_trailing",
    )(flat, ar, ac, li)


def body(matrix):
    flat = matrix.reshape(8 * 4 * NB, 128)
    ar, ac, li = gather(flat)
    return update(flat.reshape(8, 4 * NB, 128), ar, ac, li).reshape(matrix.shape)


def solution(mesh):
    spec = P(None, "row", None, None, "col", None)
    return jax.shard_map(body, mesh=mesh, in_specs=(spec,), out_specs=spec, check_vma=False)
```

```python
import jax
import jax.numpy as jnp
from jax import lax
from jax.experimental import pallas as pl
from jax.experimental.pallas import tpu as pltpu
from jax.sharding import PartitionSpec as P

F32 = jnp.float32
BF16 = jnp.bfloat16
MESH = pl.DeviceIdType.MESH
HIGHEST = lax.Precision.HIGHEST
NB = 256
LEAF = 128
CHUNKS = [(i, j) for i in range(4) for j in range(i + 1)]


def leaf_inverse(block):
    n = block.shape[0]
    sub = lax.broadcasted_iota(jnp.int32, (8, n), 0)
    lane = lax.broadcasted_iota(jnp.int32, (8, n), 1)
    rows = [block[8 * g : 8 * g + 8] for g in range(n // 8)]
    inv = [jnp.where(lane == sub + 8 * g, 1.0, 0.0).astype(F32) for g in range(n // 8)]
    out = []
    for t in range(n // 8):
        cols = [[jnp.broadcast_to(r[:, 8 * t + j : 8 * t + j + 1], (8, n)) for r in rows] for j in range(8)]
        for j in range(8):
            r = lax.rsqrt(jnp.broadcast_to(cols[j][0][j : j + 1], (8, n)))
            lcol = [c * r for c in cols[j]]
            lead = lcol[0]
            for k in range(j + 1, 8):
                f = jnp.broadcast_to(lead[k : k + 1], (8, n))
                cols[k] = [c - l * f for c, l in zip(cols[k], lcol)]
            row = jnp.broadcast_to(rows[0][j : j + 1], (8, n)) * r
            irow = jnp.broadcast_to(inv[0][j : j + 1], (8, n)) * r
            low = jnp.where(sub > j, lead, 0.0)
            rows = [rows[0] - low * row] + [a - l * row for a, l in zip(rows[1:], lcol[1:])]
            inv = [jnp.where(sub == j, irow, inv[0] - low * irow)] + [a - l * irow for a, l in zip(inv[1:], lcol[1:])]
        out.append(inv[0])
        rows, inv = rows[1:], inv[1:]
    return jnp.concatenate(out, 0)


def dot_full(a, b, trans_a=False):
    return lax.dot_general(
        a, b, (((0 if trans_a else 1,), (0,)), ((), ())), precision=HIGHEST, preferred_element_type=F32
    )


def factor_block(i, nb, d_ref, li_ref):
    n = LEAF
    s = slice(i * n, (i + 1) * n)
    m = leaf_inverse(d_ref[s, s])
    li_ref[s, s] = m
    if i:
        li_ref[s, : i * n] = -dot_full(m, d_ref[s, : i * n])
    if i + 1 < nb:
        r = dot_full(m, d_ref[s, (i + 1) * n :])
        for j in range(i + 1, nb):
            off = (j - i - 1) * n
            t = slice(j * n, (j + 1) * n)
            rj = r[:, off : off + n]
            d_ref[t, j * n :] = d_ref[t, j * n :] - dot_full(rj, r[:, off:], True)
            p = dot_full(rj, li_ref[s, : (i + 1) * n], True)
            if i:
                d_ref[t, : i * n] = d_ref[t, : i * n] + p[:, : i * n]
            d_ref[t, s] = p[:, i * n :]


def factor_first(d_ref, li_ref):
    n = LEAF
    m = leaf_inverse(d_ref[:n, :n])
    li_ref[:n, :n] = m
    r = dot_full(m, d_ref[:n, n : 2 * n])
    d_ref[:n, n : 2 * n] = r
    d_ref[n : 2 * n, n : 2 * n] = d_ref[n : 2 * n, n : 2 * n] - dot_full(r, r, True)
    d_ref[n : 2 * n, :n] = dot_full(r, m, True)


def factor_second(d_ref, li_ref):
    n = LEAF
    m = li_ref[:n, :n]
    r = dot_full(m, d_ref[:n, 2 * n :])
    d_ref[n : 2 * n, 2 * n :] = d_ref[n : 2 * n, 2 * n :] - dot_full(d_ref[:n, n : 2 * n], r, True)
    for j in (2, 3):
        rj = r[:, (j - 2) * n : (j - 1) * n]
        d_ref[j * n : (j + 1) * n, j * n :] = d_ref[j * n : (j + 1) * n, j * n :] - dot_full(rj, r[:, (j - 2) * n :], True)
        d_ref[j * n : (j + 1) * n, :n] = dot_full(rj, m, True)


def gather_kernel(x_ref, ar_ref, ac_ref, lo_ref, xin, xb, xt, d, li,
                  in_sem, loc_sem, sc_s, sc_r, zb_s, zb_r, xc_s, xc_r, cd_s, cd_r,
                  lc_s, lc_r, dg_s, dg_r, li_s, li_r):
    row = lax.axis_index("row")
    col = lax.axis_index("col")
    zl, y = row // 4, row % 4
    zh, x, co = col // 8, (col // 2) % 4, col % 2

    def dev(zl=zl, y=y, zh=zh, x=x, co=co):
        return (zl * 4 + y, (zh * 4 + x) * 2 + co)

    def rc(src, dst, ss, rs, to):
        return pltpu.make_async_remote_copy(
            src_ref=src, dst_ref=dst, send_sem=ss, recv_sem=rs, device_id=to, device_id_type=MESH
        )

    def piece(p, xq, zq):
        at = pl.multiple_of((4 * (xq // 2) + zq) * NB + (xq % 2) * LEAF, LEAF)
        return ar_ref.at[p, pl.ds(at, LEAF), :]

    top = row < 2
    root = (row == 0) & (col == 0)
    self_scatter = (row == co) & (x == 0)
    here = dev()

    load = pltpu.make_async_copy(x_ref.at[pl.ds(0, 4 * NB)], xin, in_sem)

    @pl.when(top)
    def _():
        load.start()

    bar = pltpu.get_barrier_semaphore()

    def greet(to):
        pl.semaphore_signal(bar, inc=1, device_id=to, device_id_type=MESH)

    one = lambda c: jnp.where(c, 1, 0)

    @pl.when(jnp.logical_not(self_scatter))
    def _():
        greet((co, zh * 8 + row))

    for k in range(1, 4):
        greet(dev(zh=(zh + k) % 4))
        greet(dev(x=(x + k) % 4))
    greet(dev(co=1 - co))
    edges = 7 + jnp.where(top, 4 - one(col % 8 == row), 0)
    for k in range(1, 4):
        greet(dev(y=(y + k) % 4))
    for p in range(2):

        @pl.when((row != p) & (zl == 0))
        def _():
            greet((p, col))

    edges = edges + 3 + 3 * one(top)

    @pl.when(root)
    def _():
        greet((0, 1))
        greet((1, 1))

    edges = edges + one((row < 2) & (col == 1))

    @pl.when(zl == 1)
    def _():
        greet(dev(zl=0))

    edges = edges + one(zl == 0)

    @pl.when(top)
    def _():
        load.wait()
        for q in range(4):
            v = xin[pl.ds(q, NB, stride=4), :]
            xb[:, pl.ds(q * LEAF, LEAF)] = v
            xt[pl.ds(q * LEAF, LEAF), :] = v.T

    @pl.when(root)
    def _():
        d[pl.ds(0, NB), pl.ds(0, NB)] = xb[:, pl.ds(0, NB)]
        factor_first(d, li)

    pl.semaphore_wait(bar, edges)


    def scatter(i):
        q = (x + i) % 4
        at = pl.multiple_of((4 * (q // 2) + zh) * NB + (q % 2) * LEAF, LEAF)
        return rc(xt.at[pl.ds(pl.multiple_of(q * LEAF, LEAF), LEAF)], ar_ref.at[row, pl.ds(at, LEAF), :],
                  sc_s.at[i], sc_r.at[0], (col % 8, (zh * 4 + q) * 2 + row))

    def scatter_in():
        return rc(piece(co, x, zh), piece(co, x, zh), sc_s.at[0], sc_r.at[0], dev(co=1 - co))

    def scatter_self():
        return pltpu.make_async_copy(xt.at[pl.ds(0, LEAF)], piece(co, x, zh), loc_sem.at[0])

    def z_out(k):
        q = piece(co, x, zh)
        return rc(q, q, zb_s.at[k], zb_r.at[k], dev(zh=(zh + k) % 4))

    def z_in(k):
        q = piece(co, x, (zh + 4 - k) % 4)
        return rc(q, q, zb_s.at[k], zb_r.at[k], dev(co=1 - co))

    def x_out(kz, k):
        q = piece(co, x, (zh + 4 - kz) % 4)
        return rc(q, q, xc_s.at[kz, k], xc_r.at[kz, k], dev(x=(x + (1, 3)[k]) % 4))

    def x_in(kz, k):
        q = piece(co, (x + (3, 1)[k]) % 4, (zh + 4 - kz) % 4)
        return rc(q, q, xc_s.at[kz, k], xc_r.at[kz, k], dev(co=1 - co))

    def x_relay(kz, k):
        q = piece(co, (x + (3, 1)[k]) % 4, (zh + 4 - kz) % 4).at[pl.ds(k * 64, 64)]
        return rc(q, q, xc_s.at[kz, 2 + k], xc_r.at[kz, 2 + k], dev(x=(x + (1, 3)[k]) % 4))

    def x_relay_in(kz, k):
        q = piece(co, (x + 2) % 4, (zh + 4 - kz) % 4).at[pl.ds(k * 64, 64)]
        return rc(q, q, xc_s.at[kz, 2 + k], xc_r.at[kz, 2 + k], dev(co=1 - co))

    def c_out(kz, kx):
        q = piece(co, (x + 4 - kx) % 4, (zh + 4 - kz) % 4)
        return rc(q, q, cd_s.at[kz, kx], cd_r.at[kz, kx], dev(co=1 - co))

    def c_in(kz, kx):
        q = piece(1 - co, (x + 4 - kx) % 4, (zh + 4 - kz) % 4)
        return rc(q, q, cd_s.at[kz, kx], cd_r.at[kz, kx], dev(co=1 - co))

    def lc_part(p, h):
        return ac_ref.at[pl.ds(pl.multiple_of(p * NB + h * 64, 64), 64)]

    def lc_first(p, t):
        return rc(xb.at[pl.ds(t * 64, 64)], lc_part(p, t), lc_s.at[p, t], lc_r.at[p, 0], (t, col))

    def lc_out(p, k, src=None):
        q = lc_part(p, y)
        return rc(q if src is None else src, q, lc_s.at[p, 4 + k], lc_r.at[p, k], dev(y=(y + k) % 4))

    def lc_in(p, k):
        q = lc_part(p, (y + 4 - k) % 4)
        return rc(q, q, lc_s.at[p, 4 + k], lc_r.at[p, k], dev(co=1 - co))

    def lc_cross(p, src=None):
        q = lc_part(p, y)
        return rc(q if src is None else src, q, lc_s.at[p, 4], lc_r.at[p, 0], dev(zl=1))

    def column(z, what):
        def run(cp):
            cp.start() if what == "start" else cp.wait_send()

        @pl.when(zl == z)
        def _():
            for p in range(2):
                if what == "start":
                    if z == 1:
                        lc_in(p, 0).wait_recv()
                    else:

                        @pl.when(row != p)
                        def _():
                            lc_in(p, 0).wait_recv()

                for k in range(1, 4):
                    if z == 1:
                        run(lc_out(p, k))
                    else:

                        @pl.when((row != p) & ((y + k) % 4 != p))
                        def _():
                            run(lc_out(p, k))

                        @pl.when(row == p)
                        def _():
                            run(lc_out(p, k, xb.at[pl.ds(p * 64, 64)]))

    def column_cross(what):
        for p in range(2):
            for mine in (True, False):

                @pl.when((zl == 0) & ((row == p) if mine else (row != p)))
                def _():
                    cp = lc_cross(p, xb.at[pl.ds(p * 64, 64)] if mine else None)
                    cp.start() if what == "start" else cp.wait_send()

    def column_in():
        for p in range(2):

            @pl.when(row != p)
            def _():
                for k in range(1, 4):
                    lc_in(p, k).wait_recv()

    def diag_out(p):
        return rc(xb.at[:, pl.ds(0, NB)], d.at[pl.ds(p * NB, NB), pl.ds(NB, NB)], dg_s.at[0], dg_r.at[p], (0, 0))

    def diag_in(p):
        q = d.at[pl.ds(p * NB, NB), pl.ds(NB, NB)]
        return rc(q, q, dg_s.at[0], dg_r.at[p], (0, 1))

    def li_part(ref, c):
        i, j = CHUNKS[c]
        return ref.at[pl.ds(i * LEAF, LEAF), pl.ds(j * LEAF, LEAF)]

    def li_out(c, ref, k, to):
        return rc(li_part(ref, c), li_part(lo_ref, c), li_s.at[c, k], li_r.at[c], to)

    def li_in(c):
        q = li_part(lo_ref, c)
        return rc(q, q, li_s.at[c, 0], li_r.at[c], dev(co=1 - co))

    def li_edge(c, ref, k, to, what, role):
        @pl.when(role)
        def _():
            cp = li_out(c, ref, k, to)
            cp.start() if what == "start" else cp.wait_send()

    def li_high(c, ref, what):
        mine = (row == 0) & (co == c % 2)
        for k in range(3):
            li_edge(c, ref, k, dev(x=(x + k + 1) % 4), what, mine & (zh == 0) & (x == 0))
        for k in range(2):
            li_edge(c, ref, 3 + k, dev(zh=(1, 3)[k]), what, mine & (zh == 0))
        li_edge(c, ref, 5, dev(zh=2), what, mine & (zh == 3))
        for k in range(3):
            li_edge(c, ref, 6 + k, dev(y=(y + k + 1) % 4), what, mine)

    def li_low(c, ref, what):
        mine = co == c % 2
        li_edge(c, ref, 9, dev(zl=1), what, mine & (zl == 0) & (y != 0))
        li_edge(c, ref, 6, dev(y=0), what, mine & (row == 5))
        back = mine & jnp.logical_not((row == 0) & (col == 1))
        li_edge(c, ref, 10, dev(co=1 - co), what, back if c % 2 else mine)

    def li_early(chunks):
        @pl.when((row == 0) & jnp.logical_not(root))
        def _():
            for c in chunks:
                li_in(c).wait_recv()
                li_high(c, lo_ref, "start")
                li_low(c, lo_ref, "start")

    def li_late(chunks):
        @pl.when(row != 0)
        def _():
            for c in chunks:
                li_in(c).wait_recv()
                li_low(c, lo_ref, "start")

    def li_root(i):
        @pl.when(root)
        def _():
            if i == 1:
                for p in range(2):
                    diag_in(p).wait_recv()
                factor_second(d, li)
            if i:
                factor_block(i, 4, d, li)
            for c, (a, _b) in enumerate(CHUNKS):
                if a == i:
                    if c % 2:
                        li_out(c, li, 11, dev(co=1)).start()
                    else:
                        li_high(c, li, "start")
                        li_low(c, li, "start")
                    pltpu.make_async_copy(li_part(li, c), li_part(lo_ref, c), loc_sem.at[4 + c]).start()


    for p in range(2):

        @pl.when(row == p)
        def _():
            @pl.when(col == 1)
            def _():
                diag_out(p).start()

            @pl.when(col % 8 == row)
            def _():
                scatter_self().start()

            @pl.when(col % 8 != row)
            def _():
                scatter(0).start()

            for i in range(1, 4):
                scatter(i).start()
            for t in range(4):
                if t != p:
                    lc_first(p, t).start()
            pltpu.make_async_copy(xb, ac_ref.at[pl.ds(p * NB, NB)], loc_sem.at[1]).start()

    li_root(0)
    li_root(1)


    @pl.when(self_scatter)
    def _():
        scatter_self().wait()

    @pl.when(jnp.logical_not(self_scatter))
    def _():
        scatter_in().wait_recv()

    for k in (1, 3, 2):
        z_out(k).start()
    for k in range(2):
        x_out(0, k).start()
    c_out(0, 0).start()

    li_root(2)
    li_root(3)
    li_early([0])

    def onward(kz):
        for k in range(2):
            x_out(kz, k).start()
        c_out(kz, 0).start()

    def from_x(kz):
        for k in range(2):
            x_in(kz, k).wait_recv()
            x_relay(kz, k).start()
            c_out(kz, (1, 3)[k]).start()

    def from_relay(kz):
        for k in range(2):
            x_relay_in(kz, k).wait_recv()
        c_out(kz, 2).start()

    column(0, "start")
    li_early([1, 2])
    z_in(1).wait_recv()
    onward(1)
    column_cross("start")
    for kz in (3, 2):
        z_in(kz).wait_recv()
        onward(kz)
    li_early([3, 4, 5])
    from_x(0)
    li_early([6, 7, 8, 9])
    column(1, "start")
    from_x(1)
    li_late([0, 1, 2, 3, 4, 5])
    from_x(3)
    from_x(2)
    li_late([6, 7, 8, 9])
    for kz in (0, 1, 3, 2):
        from_relay(kz)
    column_in()

    for kz in range(4):
        for kx in range(4):
            c_in(kz, kx).wait_recv()
            c_out(kz, kx).wait_send()
        for k in range(2):
            x_out(kz, k).wait_send()
            x_relay(kz, k).wait_send()

    for k in range(1, 4):
        z_out(k).wait_send()

    for p in range(2):

        @pl.when(row == p)
        def _():
            @pl.when(col == 1)
            def _():
                diag_out(p).wait_send()

            for t in range(4):
                if t != p:
                    lc_first(p, t).wait_send()
            for q in range(1, 4):
                scatter(q).wait_send()

            @pl.when(col % 8 != row)
            def _():
                scatter(0).wait_send()

            pltpu.make_async_copy(xb, ac_ref.at[pl.ds(p * NB, NB)], loc_sem.at[1]).wait()

    column(0, "wait")
    column_cross("wait")
    column(1, "wait")

    for c in range(len(CHUNKS)):

        @pl.when((row == 0) & jnp.logical_not(root & (c % 2 == 1)))
        def _():
            li_high(c, lo_ref, "wait")

        li_low(c, lo_ref, "wait")

        @pl.when(root)
        def _():
            if c % 2:
                li_out(c, li, 11, dev(co=1)).wait_send()
            pltpu.make_async_copy(li_part(li, c), li_part(lo_ref, c), loc_sem.at[4 + c]).wait()


def gather(flat):
    any_spec = pl.BlockSpec(memory_space=pl.ANY)
    dma = pltpu.SemaphoreType.DMA
    return pl.pallas_call(
        gather_kernel,
        out_shape=[
            jax.ShapeDtypeStruct((2, 2048, NB), F32),
            jax.ShapeDtypeStruct((2 * NB, 2 * NB), F32),
            jax.ShapeDtypeStruct((2 * NB, 2 * NB), F32),
        ],
        in_specs=[pl.BlockSpec(memory_space=pltpu.HBM)],
        out_specs=[any_spec] * 3,
        scratch_shapes=[
            pltpu.VMEM((4 * NB, 128), F32),
            pltpu.VMEM((NB, 2 * NB), F32),
            pltpu.VMEM((2 * NB, NB), F32),
            pltpu.VMEM((2 * NB, 2 * NB), F32),
            pltpu.VMEM((2 * NB, 2 * NB), F32),
            dma, dma((14,)),
            dma((4,)), dma((1,)),
            dma((4,)), dma((4,)),
            dma((4, 4)), dma((4, 4)),
            dma((4, 4)), dma((4, 4)),
            dma((2, 11)), dma((2, 4)),
            dma((1,)), dma((2,)),
            dma((10, 12)), dma((10,)),
        ],
        compiler_params=pltpu.CompilerParams(collective_id=0, has_side_effects=True, vmem_limit_bytes=32 << 20),
        name="gather_panel",
    )(flat)


def halves(a):
    hi = a.astype(BF16)
    return hi, (a - hi.astype(F32)).astype(BF16)


def dot3(a, b, da=1, db=0):
    mm = lambda u, v: lax.dot_general(u, v, (((da,), (db,)), ((), ())), preferred_element_type=F32)
    return mm(a[0], b[0]) + (mm(a[0], b[1]) + mm(a[1], b[0]))


def update_kernel(x_ref, ar_ref, ac_ref, li_ref, o_ref, w, a, l_hi, l_lo):
    slot = pl.program_id(0)
    row = lax.axis_index("row")
    col = lax.axis_index("col")
    kk = 2 * NB

    @pl.when(slot == 0)
    def _():
        for i in range(4):
            for j in range(4):
                at = (pl.ds(i * LEAF, LEAF), pl.ds(j * LEAF, LEAF))
                if j > i:
                    l_hi[at] = jnp.zeros((LEAF, LEAF), BF16)
                    l_lo[at] = jnp.zeros((LEAF, LEAF), BF16)
                else:
                    v = li_ref[at]
                    if i == j:
                        r = lax.broadcasted_iota(jnp.int32, v.shape, 0)
                        c = lax.broadcasted_iota(jnp.int32, v.shape, 1)
                        v = jnp.where(c <= r, v, 0.0)
                    l_hi[at], l_lo[at] = halves(v)
        l = (l_hi[...], l_lo[...])
        u = dot3(l, halves(ac_ref[...]))
        hi, lo = halves(dot3(l, halves(u), 0))
        w[pl.ds(0, kk), :] = hi
        w[pl.ds(kk, kk), :] = lo
        w[pl.ds(2 * kk, kk), :] = hi

    for p in range(2):
        hi, lo = halves(ar_ref[p])
        a[:, pl.ds(p * NB, NB)] = hi
        a[:, pl.ds(kk + p * NB, NB)] = hi
        a[:, pl.ds(2 * kk + p * NB, NB)] = lo
    grow = slot * 8 + row
    keep = grow >= 2

    def trail(half):
        upd = jnp.dot(a[...], w[:, pl.ds(half * NB, NB)], preferred_element_type=F32)
        for q in range(2):
            at = (0, pl.ds(2 * half + q, NB, stride=4), slice(None))
            o_ref[at] = jnp.where(keep, x_ref[at] - upd[:, q * LEAF : (q + 1) * LEAF], 0.0)

    trail(1)

    @pl.when((col >= 2) | ((col == 1) & (grow == 0)))
    def _():
        trail(0)

    def put(p, mask):
        n = (p + 1) * NB
        at = (pl.ds(p * NB, NB), pl.ds(0, n))
        v2 = dot3((a[:, pl.ds(0, n)], a[:, pl.ds(2 * kk, n)]), (l_hi[at], l_lo[at]), 1, 1)
        for q in range(2):
            v = v2[:, q * LEAF : (q + 1) * LEAF]
            r = lax.broadcasted_iota(jnp.int32, v.shape, 0)
            c = lax.broadcasted_iota(jnp.int32, v.shape, 1) + q * LEAF
            o_ref[0, pl.ds(q, NB, stride=4), :] = jnp.where((c <= r) | jnp.logical_not(mask), v, 0.0)

    @pl.when(col == 0)
    def _():
        put(0, grow == 0)

    @pl.when((col == 1) & (grow >= 1))
    def _():
        put(1, grow == 1)


def update(flat, ar, ac, li):
    whole = pl.BlockSpec((2 * NB, 2 * NB), lambda s: (0, 0))
    slab = pl.BlockSpec((1, 4 * NB, 128), lambda s: (s, 0, 0))
    return pl.pallas_call(
        update_kernel,
        grid=(8,),
        out_shape=jax.ShapeDtypeStruct(flat.shape, F32),
        in_specs=[slab, pl.BlockSpec((2, NB, NB), lambda s: (0, s, 0)), whole, whole],
        out_specs=slab,
        scratch_shapes=[
            pltpu.VMEM((6 * NB, 2 * NB), BF16),
            pltpu.VMEM((NB, 6 * NB), BF16),
            pltpu.VMEM((2 * NB, 2 * NB), BF16),
            pltpu.VMEM((2 * NB, 2 * NB), BF16),
        ],
        compiler_params=pltpu.CompilerParams(vmem_limit_bytes=32 << 20),
        name="update_trailing",
    )(flat, ar, ac, li)


def body(matrix):
    flat = matrix.reshape(8 * 4 * NB, 128)
    ar, ac, li = gather(flat)
    return update(flat.reshape(8, 4 * NB, 128), ar, ac, li).reshape(matrix.shape)


def solution(mesh):
    spec = P(None, "row", None, None, "col", None)
    return jax.shard_map(body, mesh=mesh, in_specs=(spec,), out_specs=spec, check_vma=False)
```

```python
import jax
import jax.numpy as jnp
from jax import lax
from jax.experimental import pallas as pl
from jax.experimental.pallas import tpu as pltpu
from jax.sharding import PartitionSpec as P

F32 = jnp.float32
BF16 = jnp.bfloat16
MESH = pl.DeviceIdType.MESH
HIGHEST = lax.Precision.HIGHEST
NB = 256
LEAF = 128
CHUNKS = [(i, j) for i in range(4) for j in range(i + 1)]
STAGES = [[0, 1, 2], [3, 4], [5, 6, 7, 8], [9]]


def leaf_inverse(block):
    n = block.shape[0]
    sub = lax.broadcasted_iota(jnp.int32, (8, n), 0)
    lane = lax.broadcasted_iota(jnp.int32, (8, n), 1)
    rows = [block[8 * g : 8 * g + 8] for g in range(n // 8)]
    inv = [jnp.where(lane == sub + 8 * g, 1.0, 0.0).astype(F32) for g in range(n // 8)]
    out = []
    for t in range(n // 8):
        cols = [[jnp.broadcast_to(r[:, 8 * t + j : 8 * t + j + 1], (8, n)) for r in rows] for j in range(8)]
        for j in range(8):
            r = lax.rsqrt(jnp.broadcast_to(cols[j][0][j : j + 1], (8, n)))
            lcol = [c * r for c in cols[j]]
            lead = lcol[0]
            for k in range(j + 1, 8):
                f = jnp.broadcast_to(lead[k : k + 1], (8, n))
                cols[k] = [c - l * f for c, l in zip(cols[k], lcol)]
            row = jnp.broadcast_to(rows[0][j : j + 1], (8, n)) * r
            irow = jnp.broadcast_to(inv[0][j : j + 1], (8, n)) * r
            low = jnp.where(sub > j, lead, 0.0)
            rows = [rows[0] - low * row] + [a - l * row for a, l in zip(rows[1:], lcol[1:])]
            inv = [jnp.where(sub == j, irow, inv[0] - low * irow)] + [a - l * irow for a, l in zip(inv[1:], lcol[1:])]
        out.append(inv[0])
        rows, inv = rows[1:], inv[1:]
    return jnp.concatenate(out, 0)


def dot_full(a, b, trans_a=False):
    return lax.dot_general(
        a, b, (((0 if trans_a else 1,), (0,)), ((), ())), precision=HIGHEST, preferred_element_type=F32
    )


def factor_block(i, nb, d_ref, li_ref):
    n = LEAF
    s = slice(i * n, (i + 1) * n)
    if i == 1:
        m = li_ref[s, s]
    else:
        m = leaf_inverse(d_ref[s, s])
        li_ref[s, s] = m
    if i + 1 < nb:
        li_ref[s, : i * n] = -dot_full(m, d_ref[s, : i * n])
        r = dot_full(m, d_ref[s, (i + 1) * n :])
        for j in range(i + 1, nb):
            off = (j - i - 1) * n
            t = slice(j * n, (j + 1) * n)
            rj = r[:, off : off + n]
            d_ref[t, j * n :] = d_ref[t, j * n :] - dot_full(rj, r[:, off:], True)
            p = dot_full(rj, li_ref[s, : (i + 1) * n], True)
            if i:
                d_ref[t, : i * n] = d_ref[t, : i * n] + p[:, : i * n]
            d_ref[t, s] = p[:, i * n :]


def factor_first(d_ref, li_ref):
    n = LEAF
    m = leaf_inverse(d_ref[:n, :n])
    li_ref[:n, :n] = m
    r = dot_full(m, d_ref[:n, n : 2 * n])
    d_ref[:n, n : 2 * n] = r
    d_ref[n : 2 * n, n : 2 * n] = d_ref[n : 2 * n, n : 2 * n] - dot_full(r, r, True)
    d_ref[n : 2 * n, :n] = dot_full(r, m, True)
    li_ref[n : 2 * n, n : 2 * n] = leaf_inverse(d_ref[n : 2 * n, n : 2 * n])


def factor_second(d_ref, li_ref):
    n = LEAF
    m = li_ref[:n, :n]
    r = dot_full(m, d_ref[:n, 2 * n :])
    d_ref[n : 2 * n, 2 * n :] = d_ref[n : 2 * n, 2 * n :] - dot_full(d_ref[:n, n : 2 * n], r, True)
    for j in (2, 3):
        rj = r[:, (j - 2) * n : (j - 1) * n]
        d_ref[j * n : (j + 1) * n, j * n :] = d_ref[j * n : (j + 1) * n, j * n :] - dot_full(rj, r[:, (j - 2) * n :], True)
        d_ref[j * n : (j + 1) * n, :n] = dot_full(rj, m, True)


def gather_kernel(x_ref, ar_ref, ac_ref, lo_ref, xin, xb, xt, d, li,
                  in_sem, loc_sem, sc_s, sc_r, zb_s, zb_r, xc_s, xc_r, cd_s, cd_r,
                  lc_s, lc_r, dg_s, dg_r, li_s, li_r):
    row = lax.axis_index("row")
    col = lax.axis_index("col")
    zl, y = row // 4, row % 4
    zh, x, co = col // 8, (col // 2) % 4, col % 2

    def dev(zl=zl, y=y, zh=zh, x=x, co=co):
        return (zl * 4 + y, (zh * 4 + x) * 2 + co)

    def rc(src, dst, ss, rs, to):
        return pltpu.make_async_remote_copy(
            src_ref=src, dst_ref=dst, send_sem=ss, recv_sem=rs, device_id=to, device_id_type=MESH
        )

    def piece(p, xq, zq):
        at = pl.multiple_of((4 * (xq // 2) + zq) * NB + (xq % 2) * LEAF, LEAF)
        return ar_ref.at[p, pl.ds(at, LEAF), :]

    top = row < 2
    root = (row == 0) & (col == 0)
    self_scatter = (row == co) & (x == 0)
    here = dev()

    load = pltpu.make_async_copy(x_ref.at[pl.ds(0, 4 * NB)], xin, in_sem)

    @pl.when(top)
    def _():
        load.start()

    bar = pltpu.get_barrier_semaphore()

    def greet(to):
        pl.semaphore_signal(bar, inc=1, device_id=to, device_id_type=MESH)

    one = lambda c: jnp.where(c, 1, 0)

    @pl.when(jnp.logical_not(self_scatter))
    def _():
        greet((co, zh * 8 + row))

    for k in range(1, 4):
        greet(dev(zh=(zh + k) % 4))
        greet(dev(x=(x + k) % 4))
    greet(dev(co=1 - co))
    edges = 7 + jnp.where(top, 4 - one(col % 8 == row), 0)
    for k in range(1, 4):
        greet(dev(y=(y + k) % 4))
    for p in range(2):

        @pl.when((row != p) & (zl == 0))
        def _():
            greet((p, col))

    edges = edges + 3 + 3 * one(top)

    @pl.when(root)
    def _():
        greet((0, 1))
        greet((1, 1))

    edges = edges + one((row < 2) & (col == 1))

    @pl.when(zl == 1)
    def _():
        greet(dev(zl=0))

    @pl.when(row == 4)
    def _():
        greet(dev(zl=0, zh=(zh + 1) % 4))

    edges = edges + one(zl == 0) + one(row == 0)

    @pl.when(top)
    def _():
        load.wait()
        for q in range(4):
            v = xin[pl.ds(q, NB, stride=4), :]
            xb[:, pl.ds(q * LEAF, LEAF)] = v
            xt[pl.ds(q * LEAF, LEAF), :] = v.T

    @pl.when(root)
    def _():
        d[pl.ds(0, NB), pl.ds(0, NB)] = xb[:, pl.ds(0, NB)]
        factor_first(d, li)

    pl.semaphore_wait(bar, edges)


    def scatter(i):
        q = (x + i) % 4
        at = pl.multiple_of((4 * (q // 2) + zh) * NB + (q % 2) * LEAF, LEAF)
        return rc(xt.at[pl.ds(pl.multiple_of(q * LEAF, LEAF), LEAF)], ar_ref.at[row, pl.ds(at, LEAF), :],
                  sc_s.at[i], sc_r.at[0], (col % 8, (zh * 4 + q) * 2 + row))

    def scatter_in():
        return rc(piece(co, x, zh), piece(co, x, zh), sc_s.at[0], sc_r.at[0], dev(co=1 - co))

    def scatter_self():
        return pltpu.make_async_copy(xt.at[pl.ds(0, LEAF)], piece(co, x, zh), loc_sem.at[0])

    def z_out(k):
        q = piece(co, x, zh)
        return rc(q, q, zb_s.at[k], zb_r.at[k], dev(zh=(zh + k) % 4))

    def z_in(k):
        q = piece(co, x, (zh + 4 - k) % 4)
        return rc(q, q, zb_s.at[k], zb_r.at[k], dev(co=1 - co))

    def x_out(kz, k):
        q = piece(co, x, (zh + 4 - kz) % 4)
        return rc(q, q, xc_s.at[kz, k], xc_r.at[kz, k], dev(x=(x + (1, 3)[k]) % 4))

    def x_in(kz, k):
        q = piece(co, (x + (3, 1)[k]) % 4, (zh + 4 - kz) % 4)
        return rc(q, q, xc_s.at[kz, k], xc_r.at[kz, k], dev(co=1 - co))

    def x_relay(kz, k):
        q = piece(co, (x + (3, 1)[k]) % 4, (zh + 4 - kz) % 4).at[pl.ds(k * 64, 64)]
        return rc(q, q, xc_s.at[kz, 2 + k], xc_r.at[kz, 2 + k], dev(x=(x + (1, 3)[k]) % 4))

    def x_relay_in(kz, k):
        q = piece(co, (x + 2) % 4, (zh + 4 - kz) % 4).at[pl.ds(k * 64, 64)]
        return rc(q, q, xc_s.at[kz, 2 + k], xc_r.at[kz, 2 + k], dev(co=1 - co))

    def c_out(kz, kx):
        q = piece(co, (x + 4 - kx) % 4, (zh + 4 - kz) % 4)
        return rc(q, q, cd_s.at[kz, kx], cd_r.at[kz, kx], dev(co=1 - co))

    def c_in(kz, kx):
        q = piece(1 - co, (x + 4 - kx) % 4, (zh + 4 - kz) % 4)
        return rc(q, q, cd_s.at[kz, kx], cd_r.at[kz, kx], dev(co=1 - co))

    def lc_part(p, h):
        return ac_ref.at[pl.ds(pl.multiple_of(p * NB + h * 64, 64), 64)]

    def lc_first(p, t):
        return rc(xb.at[pl.ds(t * 64, 64)], lc_part(p, t), lc_s.at[p, t], lc_r.at[p, 0], (t, col))

    def lc_out(p, k, src=None):
        q = lc_part(p, y)
        return rc(q if src is None else src, q, lc_s.at[p, 4 + k], lc_r.at[p, k], dev(y=(y + k) % 4))

    def lc_in(p, k):
        q = lc_part(p, (y + 4 - k) % 4)
        return rc(q, q, lc_s.at[p, 4 + k], lc_r.at[p, k], dev(co=1 - co))

    def lc_cross(p, src=None):
        q = lc_part(p, y)
        return rc(q if src is None else src, q, lc_s.at[p, 4], lc_r.at[p, 0], dev(zl=1))

    def column(z, what):
        def run(cp):
            cp.start() if what == "start" else cp.wait_send()

        @pl.when(zl == z)
        def _():
            for p in range(2):
                if what == "start":
                    if z == 1:
                        lc_in(p, 0).wait_recv()
                    else:

                        @pl.when(row != p)
                        def _():
                            lc_in(p, 0).wait_recv()

                for k in range(1, 4):
                    if z == 1:
                        run(lc_out(p, k))
                    else:

                        @pl.when((row != p) & ((y + k) % 4 != p))
                        def _():
                            run(lc_out(p, k))

                        @pl.when(row == p)
                        def _():
                            run(lc_out(p, k, xb.at[pl.ds(p * 64, 64)]))

    def column_cross(what):
        for p in range(2):
            for mine in (True, False):

                @pl.when((zl == 0) & ((row == p) if mine else (row != p)))
                def _():
                    cp = lc_cross(p, xb.at[pl.ds(p * 64, 64)] if mine else None)
                    cp.start() if what == "start" else cp.wait_send()

    def column_in():
        for p in range(2):

            @pl.when(row != p)
            def _():
                for k in range(1, 4):
                    lc_in(p, k).wait_recv()

    def diag_out(p):
        return rc(xb.at[:, pl.ds(0, NB)], d.at[pl.ds(p * NB, NB), pl.ds(NB, NB)], dg_s.at[0], dg_r.at[p], (0, 0))

    def diag_in(p):
        q = d.at[pl.ds(p * NB, NB), pl.ds(NB, NB)]
        return rc(q, q, dg_s.at[0], dg_r.at[p], (0, 1))

    def li_part(ref, c):
        i, j = CHUNKS[c]
        return ref.at[pl.ds(i * LEAF, LEAF), pl.ds(j * LEAF, LEAF)]

    def source_of(c):
        return li if CHUNKS[c][0] == CHUNKS[c][1] else d

    def li_out(c, ref, k, to):
        return rc(li_part(ref, c), li_part(lo_ref, c), li_s.at[c, k], li_r.at[c], to)

    def li_in(c):
        q = li_part(lo_ref, c)
        return rc(q, q, li_s.at[c, 0], li_r.at[c], dev(co=1 - co))

    def li_edge(c, ref, k, to, what, role):
        @pl.when(role)
        def _():
            cp = li_out(c, ref, k, to)
            cp.start() if what == "start" else cp.wait_send()

    def li_high(c, ref, what):
        mine = (row == 0) & (co == c % 2)
        for k in range(3):
            li_edge(c, ref, k, dev(x=(x + k + 1) % 4), what, mine & (zh == 0) & (x == 0))
        for k in range(2):
            li_edge(c, ref, 3 + k, dev(zh=(1, 3)[k]), what, mine & (zh == 0))
        li_edge(c, ref, 5, dev(zh=2), what, mine & (zh == 3))
        for k in range(3):
            li_edge(c, ref, 6 + k, dev(y=(y + k + 1) % 4), what, mine)

    def li_low(c, ref, what):
        mine = co == c % 2
        li_edge(c, ref, 9, dev(zl=1), what, mine & (zl == 0) & (y != 0))
        li_edge(c, ref, 9, (4, ((zh + 3) % 4 * 4 + x) * 2 + co), what, mine & (row == 0))
        back = mine & jnp.logical_not((row == 0) & (col == 1))
        li_edge(c, ref, 10, dev(co=1 - co), what, back if c % 2 else mine)

    def li_early(chunks):
        @pl.when((row == 0) & jnp.logical_not(root))
        def _():
            for c in chunks:
                li_in(c).wait_recv()
                li_high(c, lo_ref, "start")
                li_low(c, lo_ref, "start")

    def li_late(chunks):
        @pl.when(row != 0)
        def _():
            for c in chunks:
                li_in(c).wait_recv()
                li_low(c, lo_ref, "start")

    def li_root(i):
        @pl.when(root)
        def _():
            if i == 1:
                for p in range(2):
                    diag_in(p).wait_recv()
                factor_second(d, li)
            if i:
                factor_block(i, 4, d, li)
            for c in STAGES[i]:
                ref = source_of(c)
                if c % 2:
                    li_out(c, ref, 11, dev(co=1)).start()
                else:
                    li_high(c, ref, "start")
                    li_low(c, ref, "start")
                pltpu.make_async_copy(li_part(ref, c), li_part(lo_ref, c), loc_sem.at[4 + c]).start()


    for p in range(2):

        @pl.when(row == p)
        def _():
            @pl.when(col == 1)
            def _():
                diag_out(p).start()

            @pl.when(col % 8 == row)
            def _():
                scatter_self().start()

            @pl.when(col % 8 != row)
            def _():
                scatter(0).start()

            for i in range(1, 4):
                scatter(i).start()
            for t in range(4):
                if t != p:
                    lc_first(p, t).start()
            pltpu.make_async_copy(xb, ac_ref.at[pl.ds(p * NB, NB)], loc_sem.at[1]).start()

    li_root(0)
    li_root(1)


    @pl.when(self_scatter)
    def _():
        scatter_self().wait()

    @pl.when(jnp.logical_not(self_scatter))
    def _():
        scatter_in().wait_recv()

    for k in (1, 3, 2):
        z_out(k).start()
    for k in range(2):
        x_out(0, k).start()
    c_out(0, 0).start()

    li_root(2)
    li_root(3)
    li_early(STAGES[0])

    def onward(kz):
        for k in range(2):
            x_out(kz, k).start()
        c_out(kz, 0).start()

    def from_x(kz):
        for k in range(2):
            x_in(kz, k).wait_recv()
            x_relay(kz, k).start()
            c_out(kz, (1, 3)[k]).start()

    def from_relay(kz):
        for k in range(2):
            x_relay_in(kz, k).wait_recv()
        c_out(kz, 2).start()

    column(0, "start")
    li_early(STAGES[1])
    z_in(1).wait_recv()
    onward(1)
    column_cross("start")
    for kz in (3, 2):
        z_in(kz).wait_recv()
        onward(kz)
    li_early(STAGES[2])
    from_x(0)
    li_early(STAGES[3])
    column(1, "start")
    from_x(1)
    li_late(STAGES[0] + STAGES[1])
    from_x(3)
    from_x(2)
    li_late(STAGES[2] + STAGES[3])
    for kz in (0, 1, 3, 2):
        from_relay(kz)
    column_in()

    for kz in range(4):
        for kx in range(4):
            c_in(kz, kx).wait_recv()
            c_out(kz, kx).wait_send()
        for k in range(2):
            x_out(kz, k).wait_send()
            x_relay(kz, k).wait_send()

    for k in range(1, 4):
        z_out(k).wait_send()

    for p in range(2):

        @pl.when(row == p)
        def _():
            @pl.when(col == 1)
            def _():
                diag_out(p).wait_send()

            for t in range(4):
                if t != p:
                    lc_first(p, t).wait_send()
            for q in range(1, 4):
                scatter(q).wait_send()

            @pl.when(col % 8 != row)
            def _():
                scatter(0).wait_send()

            pltpu.make_async_copy(xb, ac_ref.at[pl.ds(p * NB, NB)], loc_sem.at[1]).wait()

    column(0, "wait")
    column_cross("wait")
    column(1, "wait")

    for c in range(len(CHUNKS)):

        @pl.when((row == 0) & jnp.logical_not(root & (c % 2 == 1)))
        def _():
            li_high(c, lo_ref, "wait")

        li_low(c, lo_ref, "wait")

        @pl.when(root)
        def _():
            if c % 2:
                li_out(c, source_of(c), 11, dev(co=1)).wait_send()
            pltpu.make_async_copy(li_part(source_of(c), c), li_part(lo_ref, c), loc_sem.at[4 + c]).wait()


def gather(flat):
    any_spec = pl.BlockSpec(memory_space=pl.ANY)
    dma = pltpu.SemaphoreType.DMA
    return pl.pallas_call(
        gather_kernel,
        out_shape=[
            jax.ShapeDtypeStruct((2, 2048, NB), F32),
            jax.ShapeDtypeStruct((2 * NB, 2 * NB), F32),
            jax.ShapeDtypeStruct((2 * NB, 2 * NB), F32),
        ],
        in_specs=[pl.BlockSpec(memory_space=pltpu.HBM)],
        out_specs=[any_spec] * 3,
        scratch_shapes=[
            pltpu.VMEM((4 * NB, 128), F32),
            pltpu.VMEM((NB, 2 * NB), F32),
            pltpu.VMEM((2 * NB, NB), F32),
            pltpu.VMEM((2 * NB, 2 * NB), F32),
            pltpu.VMEM((2 * NB, 2 * NB), F32),
            dma, dma((14,)),
            dma((4,)), dma((1,)),
            dma((4,)), dma((4,)),
            dma((4, 4)), dma((4, 4)),
            dma((4, 4)), dma((4, 4)),
            dma((2, 11)), dma((2, 4)),
            dma((1,)), dma((2,)),
            dma((10, 12)), dma((10,)),
        ],
        compiler_params=pltpu.CompilerParams(collective_id=0, has_side_effects=True, vmem_limit_bytes=32 << 20),
        name="gather_panel",
    )(flat)


def halves(a):
    hi = a.astype(BF16)
    return hi, (a - hi.astype(F32)).astype(BF16)


def dot3(a, b, da=1, db=0):
    mm = lambda u, v: lax.dot_general(u, v, (((da,), (db,)), ((), ())), preferred_element_type=F32)
    return mm(a[0], b[0]) + (mm(a[0], b[1]) + mm(a[1], b[0]))


def update_kernel(x_ref, ar_ref, ac_ref, li_ref, o_ref, w, a, l_hi, l_lo):
    slot = pl.program_id(0)
    row = lax.axis_index("row")
    col = lax.axis_index("col")
    kk = 2 * NB

    @pl.when(slot == 0)
    def _():
        zero = jnp.zeros((LEAF, LEAF), BF16)
        for i in range(4):
            rows = pl.ds(i * LEAF, LEAF)
            v = li_ref[rows, rows]
            r = lax.broadcasted_iota(jnp.int32, v.shape, 0)
            c = lax.broadcasted_iota(jnp.int32, v.shape, 1)
            v = jnp.where(c <= r, v, 0.0)
            l_hi[rows, rows], l_lo[rows, rows] = halves(v)
            if i:
                left = pl.ds(0, i * LEAF)
                l_hi[rows, left], l_lo[rows, left] = halves(-dot_full(v, li_ref[rows, left]))
            for j in range(i + 1, 4):
                l_hi[rows, pl.ds(j * LEAF, LEAF)] = zero
                l_lo[rows, pl.ds(j * LEAF, LEAF)] = zero
        l = (l_hi[...], l_lo[...])
        u = dot3(l, halves(ac_ref[...]))
        hi, lo = halves(dot3(l, halves(u), 0))
        w[pl.ds(0, kk), :] = hi
        w[pl.ds(kk, kk), :] = lo
        w[pl.ds(2 * kk, kk), :] = hi

    for p in range(2):
        hi, lo = halves(ar_ref[p])
        a[:, pl.ds(p * NB, NB)] = hi
        a[:, pl.ds(kk + p * NB, NB)] = hi
        a[:, pl.ds(2 * kk + p * NB, NB)] = lo
    grow = slot * 8 + row
    keep = grow >= 2

    def trail(half):
        upd = jnp.dot(a[...], w[:, pl.ds(half * NB, NB)], preferred_element_type=F32)
        for q in range(2):
            at = (0, pl.ds(2 * half + q, NB, stride=4), slice(None))
            o_ref[at] = jnp.where(keep, x_ref[at] - upd[:, q * LEAF : (q + 1) * LEAF], 0.0)

    trail(1)

    @pl.when((col >= 2) | ((col == 1) & (grow == 0)))
    def _():
        trail(0)

    def put(p, mask):
        n = (p + 1) * NB
        at = (pl.ds(p * NB, NB), pl.ds(0, n))
        v2 = dot3((a[:, pl.ds(0, n)], a[:, pl.ds(2 * kk, n)]), (l_hi[at], l_lo[at]), 1, 1)
        for q in range(2):
            v = v2[:, q * LEAF : (q + 1) * LEAF]
            r = lax.broadcasted_iota(jnp.int32, v.shape, 0)
            c = lax.broadcasted_iota(jnp.int32, v.shape, 1) + q * LEAF
            o_ref[0, pl.ds(q, NB, stride=4), :] = jnp.where((c <= r) | jnp.logical_not(mask), v, 0.0)

    @pl.when(col == 0)
    def _():
        put(0, grow == 0)

    @pl.when((col == 1) & (grow >= 1))
    def _():
        put(1, grow == 1)


def update(flat, ar, ac, li):
    whole = pl.BlockSpec((2 * NB, 2 * NB), lambda s: (0, 0))
    slab = pl.BlockSpec((1, 4 * NB, 128), lambda s: (s, 0, 0))
    return pl.pallas_call(
        update_kernel,
        grid=(8,),
        out_shape=jax.ShapeDtypeStruct(flat.shape, F32),
        in_specs=[slab, pl.BlockSpec((2, NB, NB), lambda s: (0, s, 0)), whole, whole],
        out_specs=slab,
        scratch_shapes=[
            pltpu.VMEM((6 * NB, 2 * NB), BF16),
            pltpu.VMEM((NB, 6 * NB), BF16),
            pltpu.VMEM((2 * NB, 2 * NB), BF16),
            pltpu.VMEM((2 * NB, 2 * NB), BF16),
        ],
        compiler_params=pltpu.CompilerParams(vmem_limit_bytes=32 << 20),
        name="update_trailing",
    )(flat, ar, ac, li)


def body(matrix):
    flat = matrix.reshape(8 * 4 * NB, 128)
    ar, ac, li = gather(flat)
    return update(flat.reshape(8, 4 * NB, 128), ar, ac, li).reshape(matrix.shape)


def solution(mesh):
    spec = P(None, "row", None, None, "col", None)
    return jax.shard_map(body, mesh=mesh, in_specs=(spec,), out_specs=spec, check_vma=False)
```

```python
import jax
import jax.numpy as jnp
from jax import lax
from jax.experimental import pallas as pl
from jax.experimental.pallas import tpu as pltpu
from jax.sharding import PartitionSpec as P

F32 = jnp.float32
BF16 = jnp.bfloat16
MESH = pl.DeviceIdType.MESH
HIGHEST = lax.Precision.HIGHEST
NB = 256
LEAF = 128
CHUNKS = [(i, j) for i in range(4) for j in range(i + 1)]
STAGES = [[0, 1, 2], [3, 4], [5, 6, 7, 8], [9]]


def leaf_inverse(block):
    n = block.shape[0]
    sub = lax.broadcasted_iota(jnp.int32, (8, n), 0)
    lane = lax.broadcasted_iota(jnp.int32, (8, n), 1)
    rows = [block[8 * g : 8 * g + 8] for g in range(n // 8)]
    inv = [jnp.where(lane == sub + 8 * g, 1.0, 0.0).astype(F32) for g in range(n // 8)]
    out = []
    for t in range(n // 8):
        cols = [[jnp.broadcast_to(r[:, 8 * t + j : 8 * t + j + 1], (8, n)) for r in rows] for j in range(8)]
        for j in range(8):
            r = lax.rsqrt(jnp.broadcast_to(cols[j][0][j : j + 1], (8, n)))
            lcol = [c * r for c in cols[j]]
            lead = lcol[0]
            for k in range(j + 1, 8):
                f = jnp.broadcast_to(lead[k : k + 1], (8, n))
                cols[k] = [c - l * f for c, l in zip(cols[k], lcol)]
            row = jnp.broadcast_to(rows[0][j : j + 1], (8, n)) * r
            irow = jnp.broadcast_to(inv[0][j : j + 1], (8, n)) * r
            low = jnp.where(sub > j, lead, 0.0)
            rows = [rows[0] - low * row] + [a - l * row for a, l in zip(rows[1:], lcol[1:])]
            inv = [jnp.where(sub == j, irow, inv[0] - low * irow)] + [a - l * irow for a, l in zip(inv[1:], lcol[1:])]
        out.append(inv[0])
        rows, inv = rows[1:], inv[1:]
    return jnp.concatenate(out, 0)


def dot_full(a, b, trans_a=False):
    return lax.dot_general(
        a, b, (((0 if trans_a else 1,), (0,)), ((), ())), precision=HIGHEST, preferred_element_type=F32
    )


def factor_block(i, nb, d_ref, li_ref):
    n = LEAF
    s = slice(i * n, (i + 1) * n)
    if i == 1:
        m = li_ref[s, s]
    else:
        m = leaf_inverse(d_ref[s, s])
        li_ref[s, s] = m
    if i + 1 < nb:
        li_ref[s, : i * n] = -dot_full(m, d_ref[s, : i * n])
        r = dot_full(m, d_ref[s, (i + 1) * n :])
        for j in range(i + 1, nb):
            off = (j - i - 1) * n
            t = slice(j * n, (j + 1) * n)
            rj = r[:, off : off + n]
            d_ref[t, j * n :] = d_ref[t, j * n :] - dot_full(rj, r[:, off:], True)
            p = dot_full(rj, li_ref[s, : (i + 1) * n], True)
            if i:
                d_ref[t, : i * n] = d_ref[t, : i * n] + p[:, : i * n]
            d_ref[t, s] = p[:, i * n :]


def factor_first(d_ref, li_ref):
    n = LEAF
    m = leaf_inverse(d_ref[:n, :n])
    li_ref[:n, :n] = m
    r = dot_full(m, d_ref[:n, n : 2 * n])
    d_ref[:n, n : 2 * n] = r
    d_ref[n : 2 * n, n : 2 * n] = d_ref[n : 2 * n, n : 2 * n] - dot_full(r, r, True)
    d_ref[n : 2 * n, :n] = dot_full(r, m, True)
    li_ref[n : 2 * n, n : 2 * n] = leaf_inverse(d_ref[n : 2 * n, n : 2 * n])


def factor_second(d_ref, li_ref):
    n = LEAF
    m = li_ref[:n, :n]
    r = dot_full(m, d_ref[:n, 2 * n :])
    d_ref[n : 2 * n, 2 * n :] = d_ref[n : 2 * n, 2 * n :] - dot_full(d_ref[:n, n : 2 * n], r, True)
    for j in (2, 3):
        rj = r[:, (j - 2) * n : (j - 1) * n]
        d_ref[j * n : (j + 1) * n, j * n :] = d_ref[j * n : (j + 1) * n, j * n :] - dot_full(rj, r[:, (j - 2) * n :], True)
        d_ref[j * n : (j + 1) * n, :n] = dot_full(rj, m, True)


def gather_kernel(x_ref, ar_ref, ac_ref, lo_ref, xin, xb, xt, d, li,
                  in_sem, loc_sem, sc_s, sc_r, zb_s, zb_r, xc_s, xc_r, cd_s, cd_r,
                  lc_s, lc_r, dg_s, dg_r, li_s, li_r):
    row = lax.axis_index("row")
    col = lax.axis_index("col")
    zl, y = row // 4, row % 4
    zh, x, co = col // 8, (col // 2) % 4, col % 2

    def dev(zl=zl, y=y, zh=zh, x=x, co=co):
        return (zl * 4 + y, (zh * 4 + x) * 2 + co)

    def rc(src, dst, ss, rs, to):
        return pltpu.make_async_remote_copy(
            src_ref=src, dst_ref=dst, send_sem=ss, recv_sem=rs, device_id=to, device_id_type=MESH
        )

    def piece(p, xq, zq):
        at = pl.multiple_of((4 * (xq // 2) + zq) * NB + (xq % 2) * LEAF, LEAF)
        return ar_ref.at[p, pl.ds(at, LEAF), :]

    top = row < 2
    root = (row == 0) & (col == 0)
    self_scatter = (row == co) & (x == 0)
    here = dev()

    load = pltpu.make_async_copy(x_ref.at[pl.ds(0, 4 * NB)], xin, in_sem)

    @pl.when(top)
    def _():
        load.start()

    bar = pltpu.get_barrier_semaphore()

    def greet(to):
        pl.semaphore_signal(bar, inc=1, device_id=to, device_id_type=MESH)

    one = lambda c: jnp.where(c, 1, 0)

    @pl.when(jnp.logical_not(self_scatter))
    def _():
        greet((co, zh * 8 + row))

    for k in range(1, 4):
        greet(dev(zh=(zh + k) % 4))
        greet(dev(x=(x + k) % 4))
    greet(dev(co=1 - co))
    edges = 7 + jnp.where(top, 4 - one(col % 8 == row), 0)
    for k in range(1, 4):
        greet(dev(y=(y + k) % 4))
    for p in range(2):

        @pl.when((row != p) & (zl == 0))
        def _():
            greet((p, col))

    edges = edges + 3 + 3 * one(top)

    @pl.when(root)
    def _():
        greet((0, 1))
        greet((1, 1))

    edges = edges + one((row < 2) & (col == 1))

    @pl.when(zl == 1)
    def _():
        greet(dev(zl=0))

    @pl.when(row == 4)
    def _():
        greet(dev(zl=0, zh=(zh + 1) % 4))

    edges = edges + one(zl == 0) + one(row == 0)

    @pl.when(top)
    def _():
        load.wait()
        for q in range(4):
            v = xin[pl.ds(q, NB, stride=4), :]
            xb[:, pl.ds(q * LEAF, LEAF)] = v
            xt[pl.ds(q * LEAF, LEAF), :] = v.T

    @pl.when(root)
    def _():
        d[pl.ds(0, NB), pl.ds(0, NB)] = xb[:, pl.ds(0, NB)]
        factor_first(d, li)

    pl.semaphore_wait(bar, edges)


    def scatter(i):
        q = (x + i) % 4
        at = pl.multiple_of((4 * (q // 2) + zh) * NB + (q % 2) * LEAF, LEAF)
        return rc(xt.at[pl.ds(pl.multiple_of(q * LEAF, LEAF), LEAF)], ar_ref.at[row, pl.ds(at, LEAF), :],
                  sc_s.at[i], sc_r.at[0], (col % 8, (zh * 4 + q) * 2 + row))

    def scatter_in():
        return rc(piece(co, x, zh), piece(co, x, zh), sc_s.at[0], sc_r.at[0], dev(co=1 - co))

    def scatter_self():
        return pltpu.make_async_copy(xt.at[pl.ds(0, LEAF)], piece(co, x, zh), loc_sem.at[0])

    def z_out(k):
        q = piece(co, x, zh)
        return rc(q, q, zb_s.at[k], zb_r.at[k], dev(zh=(zh + k) % 4))

    def z_in(k):
        q = piece(co, x, (zh + 4 - k) % 4)
        return rc(q, q, zb_s.at[k], zb_r.at[k], dev(co=1 - co))

    def x_out(kz, k):
        q = piece(co, x, (zh + 4 - kz) % 4)
        return rc(q, q, xc_s.at[kz, k], xc_r.at[kz, k], dev(x=(x + (1, 3)[k]) % 4))

    def x_in(kz, k):
        q = piece(co, (x + (3, 1)[k]) % 4, (zh + 4 - kz) % 4)
        return rc(q, q, xc_s.at[kz, k], xc_r.at[kz, k], dev(co=1 - co))

    def x_relay(kz, k):
        q = piece(co, (x + (3, 1)[k]) % 4, (zh + 4 - kz) % 4).at[pl.ds(k * 64, 64)]
        return rc(q, q, xc_s.at[kz, 2 + k], xc_r.at[kz, 2 + k], dev(x=(x + (1, 3)[k]) % 4))

    def x_relay_in(kz, k):
        q = piece(co, (x + 2) % 4, (zh + 4 - kz) % 4).at[pl.ds(k * 64, 64)]
        return rc(q, q, xc_s.at[kz, 2 + k], xc_r.at[kz, 2 + k], dev(co=1 - co))

    def c_out(kz, kx):
        q = piece(co, (x + 4 - kx) % 4, (zh + 4 - kz) % 4)
        return rc(q, q, cd_s.at[kz, kx], cd_r.at[kz, kx], dev(co=1 - co))

    def c_in(kz, kx):
        q = piece(1 - co, (x + 4 - kx) % 4, (zh + 4 - kz) % 4)
        return rc(q, q, cd_s.at[kz, kx], cd_r.at[kz, kx], dev(co=1 - co))

    def lc_part(p, h):
        return ac_ref.at[pl.ds(pl.multiple_of(p * NB + h * 64, 64), 64)]

    def lc_first(p, t):
        return rc(xb.at[pl.ds(t * 64, 64)], lc_part(p, t), lc_s.at[p, t], lc_r.at[p, 0], (t, col))

    def lc_out(p, k, src=None):
        q = lc_part(p, y)
        return rc(q if src is None else src, q, lc_s.at[p, 4 + k], lc_r.at[p, k], dev(y=(y + k) % 4))

    def lc_in(p, k):
        q = lc_part(p, (y + 4 - k) % 4)
        return rc(q, q, lc_s.at[p, 4 + k], lc_r.at[p, k], dev(co=1 - co))

    def lc_cross(p, src=None):
        q = lc_part(p, y)
        return rc(q if src is None else src, q, lc_s.at[p, 4], lc_r.at[p, 0], dev(zl=1))

    def column(z, what):
        def run(cp):
            cp.start() if what == "start" else cp.wait_send()

        @pl.when(zl == z)
        def _():
            for p in range(2):
                if what == "start":
                    if z == 1:
                        lc_in(p, 0).wait_recv()
                    else:

                        @pl.when(row != p)
                        def _():
                            lc_in(p, 0).wait_recv()

                for k in range(1, 4):
                    if z == 1:
                        run(lc_out(p, k))
                    else:

                        @pl.when((row != p) & ((y + k) % 4 != p))
                        def _():
                            run(lc_out(p, k))

                        @pl.when(row == p)
                        def _():
                            run(lc_out(p, k, xb.at[pl.ds(p * 64, 64)]))

    def column_cross(what):
        for p in range(2):
            for mine in (True, False):

                @pl.when((zl == 0) & ((row == p) if mine else (row != p)))
                def _():
                    cp = lc_cross(p, xb.at[pl.ds(p * 64, 64)] if mine else None)
                    cp.start() if what == "start" else cp.wait_send()

    def column_in():
        for p in range(2):

            @pl.when(row != p)
            def _():
                for k in range(1, 4):
                    lc_in(p, k).wait_recv()

    def diag_out(p):
        return rc(xb.at[:, pl.ds(0, NB)], d.at[pl.ds(p * NB, NB), pl.ds(NB, NB)], dg_s.at[0], dg_r.at[p], (0, 0))

    def diag_in(p):
        q = d.at[pl.ds(p * NB, NB), pl.ds(NB, NB)]
        return rc(q, q, dg_s.at[0], dg_r.at[p], (0, 1))

    def li_part(ref, c):
        i, j = CHUNKS[c]
        return ref.at[pl.ds(i * LEAF, LEAF), pl.ds(j * LEAF, LEAF)]

    def source_of(c):
        return li if CHUNKS[c][0] == CHUNKS[c][1] else d

    def li_out(c, ref, k, to):
        return rc(li_part(ref, c), li_part(lo_ref, c), li_s.at[c, k], li_r.at[c], to)

    def li_in(c):
        q = li_part(lo_ref, c)
        return rc(q, q, li_s.at[c, 0], li_r.at[c], dev(co=1 - co))

    def li_edge(c, ref, k, to, what, role):
        @pl.when(role)
        def _():
            cp = li_out(c, ref, k, to)
            cp.start() if what == "start" else cp.wait_send()

    def li_high(c, ref, what):
        mine = (row == 0) & (co == c % 2)
        for k in range(3):
            li_edge(c, ref, k, dev(x=(x + k + 1) % 4), what, mine & (zh == 0) & (x == 0))
        for k in range(2):
            li_edge(c, ref, 3 + k, dev(zh=(1, 3)[k]), what, mine & (zh == 0))
        li_edge(c, ref, 5, dev(zh=2), what, mine & (zh == 3))
        for k in (0, 2):
            li_edge(c, ref, 6 + k, dev(y=(y + k + 1) % 4), what, mine)

    def li_low(c, ref, what):
        mine = co == c % 2
        li_edge(c, ref, 7, dev(y=2), what, mine & (row == 3))
        li_edge(c, ref, 9, dev(zl=1), what, mine & (zl == 0) & (y != 0))
        li_edge(c, ref, 9, (4, ((zh + 3) % 4 * 4 + x) * 2 + co), what, mine & (row == 0))
        back = mine & jnp.logical_not((row == 0) & (col == 1))
        li_edge(c, ref, 10, dev(co=1 - co), what, back if c % 2 else mine)

    def li_early(chunks):
        @pl.when((row == 0) & jnp.logical_not(root))
        def _():
            for c in chunks:
                li_in(c).wait_recv()
                li_high(c, lo_ref, "start")
                li_low(c, lo_ref, "start")

    def li_late(chunks):
        @pl.when(row != 0)
        def _():
            for c in chunks:
                li_in(c).wait_recv()
                li_low(c, lo_ref, "start")

    def li_root(i):
        @pl.when(root)
        def _():
            if i == 1:
                for p in range(2):
                    diag_in(p).wait_recv()
                factor_second(d, li)
            if i:
                factor_block(i, 4, d, li)
            for c in STAGES[i]:
                ref = source_of(c)
                if c % 2:
                    li_out(c, ref, 11, dev(co=1)).start()
                else:
                    li_high(c, ref, "start")
                    li_low(c, ref, "start")
                pltpu.make_async_copy(li_part(ref, c), li_part(lo_ref, c), loc_sem.at[4 + c]).start()


    for p in range(2):

        @pl.when(row == p)
        def _():
            @pl.when(col == 1)
            def _():
                diag_out(p).start()

            @pl.when(col % 8 == row)
            def _():
                scatter_self().start()

            @pl.when(col % 8 != row)
            def _():
                scatter(0).start()

            for i in range(1, 4):
                scatter(i).start()
            for t in range(4):
                if t != p:
                    lc_first(p, t).start()
            pltpu.make_async_copy(xb, ac_ref.at[pl.ds(p * NB, NB)], loc_sem.at[1]).start()

    li_root(0)
    li_root(1)


    @pl.when(self_scatter)
    def _():
        scatter_self().wait()

    @pl.when(jnp.logical_not(self_scatter))
    def _():
        scatter_in().wait_recv()

    for k in (1, 3, 2):
        z_out(k).start()
    for k in range(2):
        x_out(0, k).start()
    c_out(0, 0).start()

    li_root(2)
    li_root(3)
    li_early(STAGES[0])

    def onward(kz):
        for k in range(2):
            x_out(kz, k).start()
        c_out(kz, 0).start()

    def from_x(kz):
        for k in range(2):
            x_in(kz, k).wait_recv()
            x_relay(kz, k).start()
            c_out(kz, (1, 3)[k]).start()

    def from_relay(kz):
        for k in range(2):
            x_relay_in(kz, k).wait_recv()
        c_out(kz, 2).start()

    column(0, "start")
    li_early(STAGES[1])
    z_in(1).wait_recv()
    onward(1)
    column_cross("start")
    for kz in (3, 2):
        z_in(kz).wait_recv()
        onward(kz)
    li_early(STAGES[2])
    from_x(0)
    li_early(STAGES[3])
    column(1, "start")
    from_x(1)
    li_late(STAGES[0] + STAGES[1])
    from_x(3)
    from_x(2)
    li_late(STAGES[2] + STAGES[3])
    for kz in (0, 1, 3, 2):
        from_relay(kz)
    column_in()

    for kz in range(4):
        for kx in range(4):
            c_in(kz, kx).wait_recv()
            c_out(kz, kx).wait_send()
        for k in range(2):
            x_out(kz, k).wait_send()
            x_relay(kz, k).wait_send()

    for k in range(1, 4):
        z_out(k).wait_send()

    for p in range(2):

        @pl.when(row == p)
        def _():
            @pl.when(col == 1)
            def _():
                diag_out(p).wait_send()

            for t in range(4):
                if t != p:
                    lc_first(p, t).wait_send()
            for q in range(1, 4):
                scatter(q).wait_send()

            @pl.when(col % 8 != row)
            def _():
                scatter(0).wait_send()

            pltpu.make_async_copy(xb, ac_ref.at[pl.ds(p * NB, NB)], loc_sem.at[1]).wait()

    column(0, "wait")
    column_cross("wait")
    column(1, "wait")

    for c in range(len(CHUNKS)):

        @pl.when((row == 0) & jnp.logical_not(root & (c % 2 == 1)))
        def _():
            li_high(c, lo_ref, "wait")

        li_low(c, lo_ref, "wait")

        @pl.when(root)
        def _():
            if c % 2:
                li_out(c, source_of(c), 11, dev(co=1)).wait_send()
            pltpu.make_async_copy(li_part(source_of(c), c), li_part(lo_ref, c), loc_sem.at[4 + c]).wait()


def gather(flat):
    any_spec = pl.BlockSpec(memory_space=pl.ANY)
    dma = pltpu.SemaphoreType.DMA
    return pl.pallas_call(
        gather_kernel,
        out_shape=[
            jax.ShapeDtypeStruct((2, 2048, NB), F32),
            jax.ShapeDtypeStruct((2 * NB, 2 * NB), F32),
            jax.ShapeDtypeStruct((2 * NB, 2 * NB), F32),
        ],
        in_specs=[pl.BlockSpec(memory_space=pltpu.HBM)],
        out_specs=[any_spec] * 3,
        scratch_shapes=[
            pltpu.VMEM((4 * NB, 128), F32),
            pltpu.VMEM((NB, 2 * NB), F32),
            pltpu.VMEM((2 * NB, NB), F32),
            pltpu.VMEM((2 * NB, 2 * NB), F32),
            pltpu.VMEM((2 * NB, 2 * NB), F32),
            dma, dma((14,)),
            dma((4,)), dma((1,)),
            dma((4,)), dma((4,)),
            dma((4, 4)), dma((4, 4)),
            dma((4, 4)), dma((4, 4)),
            dma((2, 11)), dma((2, 4)),
            dma((1,)), dma((2,)),
            dma((10, 12)), dma((10,)),
        ],
        compiler_params=pltpu.CompilerParams(collective_id=0, has_side_effects=True, vmem_limit_bytes=32 << 20),
        name="gather_panel",
    )(flat)


def halves(a):
    hi = a.astype(BF16)
    return hi, (a - hi.astype(F32)).astype(BF16)


def dot3(a, b, da=1, db=0):
    mm = lambda u, v: lax.dot_general(u, v, (((da,), (db,)), ((), ())), preferred_element_type=F32)
    return mm(a[0], b[0]) + (mm(a[0], b[1]) + mm(a[1], b[0]))


def update_kernel(x_ref, ar_ref, ac_ref, li_ref, o_ref, w, a, l_hi, l_lo):
    slot = pl.program_id(0)
    row = lax.axis_index("row")
    col = lax.axis_index("col")
    kk = 2 * NB

    @pl.when(slot == 0)
    def _():
        zero = jnp.zeros((LEAF, LEAF), BF16)
        for i in range(4):
            rows = pl.ds(i * LEAF, LEAF)
            v = li_ref[rows, rows]
            r = lax.broadcasted_iota(jnp.int32, v.shape, 0)
            c = lax.broadcasted_iota(jnp.int32, v.shape, 1)
            v = jnp.where(c <= r, v, 0.0)
            l_hi[rows, rows], l_lo[rows, rows] = halves(v)
            if i:
                left = pl.ds(0, i * LEAF)
                l_hi[rows, left], l_lo[rows, left] = halves(-dot_full(v, li_ref[rows, left]))
            for j in range(i + 1, 4):
                l_hi[rows, pl.ds(j * LEAF, LEAF)] = zero
                l_lo[rows, pl.ds(j * LEAF, LEAF)] = zero
        l = (l_hi[...], l_lo[...])
        u = dot3(l, halves(ac_ref[...]))
        hi, lo = halves(dot3(l, halves(u), 0))
        w[pl.ds(0, kk), :] = hi
        w[pl.ds(kk, kk), :] = lo
        w[pl.ds(2 * kk, kk), :] = hi

    for p in range(2):
        hi, lo = halves(ar_ref[p])
        a[:, pl.ds(p * NB, NB)] = hi
        a[:, pl.ds(kk + p * NB, NB)] = hi
        a[:, pl.ds(2 * kk + p * NB, NB)] = lo
    grow = slot * 8 + row
    keep = grow >= 2

    def trail(half):
        upd = jnp.dot(a[...], w[:, pl.ds(half * NB, NB)], preferred_element_type=F32)
        for q in range(2):
            at = (0, pl.ds(2 * half + q, NB, stride=4), slice(None))
            o_ref[at] = jnp.where(keep, x_ref[at] - upd[:, q * LEAF : (q + 1) * LEAF], 0.0)

    trail(1)

    @pl.when((col >= 2) | ((col == 1) & (grow == 0)))
    def _():
        trail(0)

    def put(p, mask):
        n = (p + 1) * NB
        at = (pl.ds(p * NB, NB), pl.ds(0, n))
        v2 = dot3((a[:, pl.ds(0, n)], a[:, pl.ds(2 * kk, n)]), (l_hi[at], l_lo[at]), 1, 1)
        for q in range(2):
            v = v2[:, q * LEAF : (q + 1) * LEAF]
            r = lax.broadcasted_iota(jnp.int32, v.shape, 0)
            c = lax.broadcasted_iota(jnp.int32, v.shape, 1) + q * LEAF
            o_ref[0, pl.ds(q, NB, stride=4), :] = jnp.where((c <= r) | jnp.logical_not(mask), v, 0.0)

    @pl.when(col == 0)
    def _():
        put(0, grow == 0)

    @pl.when((col == 1) & (grow >= 1))
    def _():
        put(1, grow == 1)


def update(flat, ar, ac, li):
    whole = pl.BlockSpec((2 * NB, 2 * NB), lambda s: (0, 0))
    slab = pl.BlockSpec((1, 4 * NB, 128), lambda s: (s, 0, 0))
    return pl.pallas_call(
        update_kernel,
        grid=(8,),
        out_shape=jax.ShapeDtypeStruct(flat.shape, F32),
        in_specs=[slab, pl.BlockSpec((2, NB, NB), lambda s: (0, s, 0)), whole, whole],
        out_specs=slab,
        scratch_shapes=[
            pltpu.VMEM((6 * NB, 2 * NB), BF16),
            pltpu.VMEM((NB, 6 * NB), BF16),
            pltpu.VMEM((2 * NB, 2 * NB), BF16),
            pltpu.VMEM((2 * NB, 2 * NB), BF16),
        ],
        compiler_params=pltpu.CompilerParams(vmem_limit_bytes=32 << 20),
        name="update_trailing",
    )(flat, ar, ac, li)


def body(matrix):
    flat = matrix.reshape(8 * 4 * NB, 128)
    ar, ac, li = gather(flat)
    return update(flat.reshape(8, 4 * NB, 128), ar, ac, li).reshape(matrix.shape)


def solution(mesh):
    spec = P(None, "row", None, None, "col", None)
    return jax.shard_map(body, mesh=mesh, in_specs=(spec,), out_specs=spec, check_vma=False)
```

```python
import jax
import jax.numpy as jnp
from jax import lax
from jax.experimental import pallas as pl
from jax.experimental.pallas import tpu as pltpu
from jax.sharding import PartitionSpec as P

F32 = jnp.float32
BF16 = jnp.bfloat16
MESH = pl.DeviceIdType.MESH
HIGHEST = lax.Precision.HIGHEST
NB = 256
LEAF = 128
CHUNKS = [(i, j) for i in range(4) for j in range(i + 1)]
STAGES = [[0, 1, 2], [3, 4], [5, 6, 7, 8], [9]]


def leaf_inverse(block):
    n = block.shape[0]
    sub = lax.broadcasted_iota(jnp.int32, (8, n), 0)
    lane = lax.broadcasted_iota(jnp.int32, (8, n), 1)
    rows = [block[8 * g : 8 * g + 8] for g in range(n // 8)]
    inv = [jnp.where(lane == sub + 8 * g, 1.0, 0.0).astype(F32) for g in range(n // 8)]
    out = []
    for t in range(n // 8):
        cols = [[jnp.broadcast_to(r[:, 8 * t + j : 8 * t + j + 1], (8, n)) for r in rows] for j in range(8)]
        for j in range(8):
            r = lax.rsqrt(jnp.broadcast_to(cols[j][0][j : j + 1], (8, n)))
            lcol = [c * r for c in cols[j]]
            lead = lcol[0]
            for k in range(j + 1, 8):
                f = jnp.broadcast_to(lead[k : k + 1], (8, n))
                cols[k] = [c - l * f for c, l in zip(cols[k], lcol)]
            row = jnp.broadcast_to(rows[0][j : j + 1], (8, n)) * r
            irow = jnp.broadcast_to(inv[0][j : j + 1], (8, n)) * r
            low = jnp.where(sub > j, lead, 0.0)
            rows = [rows[0] - low * row] + [a - l * row for a, l in zip(rows[1:], lcol[1:])]
            inv = [jnp.where(sub == j, irow, inv[0] - low * irow)] + [a - l * irow for a, l in zip(inv[1:], lcol[1:])]
        out.append(inv[0])
        rows, inv = rows[1:], inv[1:]
    return jnp.concatenate(out, 0)


def dot_full(a, b, trans_a=False):
    return lax.dot_general(
        a, b, (((0 if trans_a else 1,), (0,)), ((), ())), precision=HIGHEST, preferred_element_type=F32
    )


def factor_block(i, nb, d_ref, li_ref):
    n = LEAF
    s = slice(i * n, (i + 1) * n)
    if i == 1:
        m = li_ref[s, s]
    else:
        m = leaf_inverse(d_ref[s, s])
        li_ref[s, s] = m
    if i + 1 < nb:
        li_ref[s, : i * n] = -dot_full(m, d_ref[s, : i * n])
        r = dot_full(m, d_ref[s, (i + 1) * n :])
        for j in range(i + 1, nb):
            off = (j - i - 1) * n
            t = slice(j * n, (j + 1) * n)
            rj = r[:, off : off + n]
            d_ref[t, j * n :] = d_ref[t, j * n :] - dot_full(rj, r[:, off:], True)
            p = dot_full(rj, li_ref[s, : (i + 1) * n], True)
            if i:
                d_ref[t, : i * n] = d_ref[t, : i * n] + p[:, : i * n]
            d_ref[t, s] = p[:, i * n :]


def factor_first(d_ref, li_ref):
    n = LEAF
    m = leaf_inverse(d_ref[:n, :n])
    li_ref[:n, :n] = m
    r = dot_full(m, d_ref[:n, n : 2 * n])
    d_ref[:n, n : 2 * n] = r
    d_ref[n : 2 * n, n : 2 * n] = d_ref[n : 2 * n, n : 2 * n] - dot_full(r, r, True)
    d_ref[n : 2 * n, :n] = dot_full(r, m, True)
    li_ref[n : 2 * n, n : 2 * n] = leaf_inverse(d_ref[n : 2 * n, n : 2 * n])


def factor_second(d_ref, li_ref):
    n = LEAF
    m = li_ref[:n, :n]
    r = dot_full(m, d_ref[:n, 2 * n :])
    d_ref[n : 2 * n, 2 * n :] = d_ref[n : 2 * n, 2 * n :] - dot_full(d_ref[:n, n : 2 * n], r, True)
    for j in (2, 3):
        rj = r[:, (j - 2) * n : (j - 1) * n]
        d_ref[j * n : (j + 1) * n, j * n :] = d_ref[j * n : (j + 1) * n, j * n :] - dot_full(rj, r[:, (j - 2) * n :], True)
        d_ref[j * n : (j + 1) * n, :n] = dot_full(rj, m, True)


def gather_kernel(x_ref, ar_ref, ac_ref, lo_ref, xin, xb, xt, d, li,
                  in_sem, loc_sem, sc_s, sc_r, zb_s, zb_r, xc_s, xc_r, cd_s, cd_r,
                  lc_s, lc_r, dg_s, dg_r, li_s, li_r):
    row = lax.axis_index("row")
    col = lax.axis_index("col")
    zl, y = row // 4, row % 4
    zh, x, co = col // 8, (col // 2) % 4, col % 2

    def dev(zl=zl, y=y, zh=zh, x=x, co=co):
        return (zl * 4 + y, (zh * 4 + x) * 2 + co)

    def rc(src, dst, ss, rs, to):
        return pltpu.make_async_remote_copy(
            src_ref=src, dst_ref=dst, send_sem=ss, recv_sem=rs, device_id=to, device_id_type=MESH
        )

    def piece(p, xq, zq):
        at = pl.multiple_of((4 * (xq // 2) + zq) * NB + (xq % 2) * LEAF, LEAF)
        return ar_ref.at[p, pl.ds(at, LEAF), :]

    top = row < 2
    root = (row == 0) & (col == 0)
    self_scatter = (row == co) & (x == 0)
    here = dev()

    load = pltpu.make_async_copy(x_ref.at[pl.ds(0, 4 * NB)], xin, in_sem)

    @pl.when(top)
    def _():
        load.start()

    bar = pltpu.get_barrier_semaphore()

    def greet(to):
        pl.semaphore_signal(bar, inc=1, device_id=to, device_id_type=MESH)

    one = lambda c: jnp.where(c, 1, 0)

    @pl.when(jnp.logical_not(self_scatter))
    def _():
        greet((co, zh * 8 + row))

    for k in range(1, 4):
        greet(dev(zh=(zh + k) % 4))
        greet(dev(x=(x + k) % 4))
    greet(dev(co=1 - co))
    edges = 7 + jnp.where(top, 4 - one(col % 8 == row), 0)
    for k in range(1, 4):
        greet(dev(y=(y + k) % 4))
    for p in range(2):

        @pl.when((row != p) & (zl == 0))
        def _():
            greet((p, col))

    edges = edges + 3 + 3 * one(top)

    @pl.when(root)
    def _():
        greet((0, 1))
        greet((1, 1))

    edges = edges + one((row < 2) & (col == 1))

    @pl.when(zl == 1)
    def _():
        greet(dev(zl=0))

    @pl.when(row == 4)
    def _():
        greet(dev(zl=0, zh=(zh + 1) % 4))

    edges = edges + one(zl == 0) + one(row == 0)

    @pl.when(top)
    def _():
        load.wait()
        for q in range(4):
            v = xin[pl.ds(q, NB, stride=4), :]
            xb[:, pl.ds(q * LEAF, LEAF)] = v
            xt[pl.ds(q * LEAF, LEAF), :] = v.T

    @pl.when(root)
    def _():
        d[pl.ds(0, NB), pl.ds(0, NB)] = xb[:, pl.ds(0, NB)]
        factor_first(d, li)

    pl.semaphore_wait(bar, edges)


    def scatter(i):
        q = (x + i) % 4
        at = pl.multiple_of((4 * (q // 2) + zh) * NB + (q % 2) * LEAF, LEAF)
        return rc(xt.at[pl.ds(pl.multiple_of(q * LEAF, LEAF), LEAF)], ar_ref.at[row, pl.ds(at, LEAF), :],
                  sc_s.at[i], sc_r.at[0], (col % 8, (zh * 4 + q) * 2 + row))

    def scatter_in():
        return rc(piece(co, x, zh), piece(co, x, zh), sc_s.at[0], sc_r.at[0], dev(co=1 - co))

    def scatter_self():
        return pltpu.make_async_copy(xt.at[pl.ds(0, LEAF)], piece(co, x, zh), loc_sem.at[0])

    def z_out(k):
        q = piece(co, x, zh)
        return rc(q, q, zb_s.at[k], zb_r.at[k], dev(zh=(zh + k) % 4))

    def z_in(k):
        q = piece(co, x, (zh + 4 - k) % 4)
        return rc(q, q, zb_s.at[k], zb_r.at[k], dev(co=1 - co))

    def x_out(kz, k):
        q = piece(co, x, (zh + 4 - kz) % 4)
        return rc(q, q, xc_s.at[kz, k], xc_r.at[kz, k], dev(x=(x + (1, 3)[k]) % 4))

    def x_in(kz, k):
        q = piece(co, (x + (3, 1)[k]) % 4, (zh + 4 - kz) % 4)
        return rc(q, q, xc_s.at[kz, k], xc_r.at[kz, k], dev(co=1 - co))

    def x_relay(kz, k):
        q = piece(co, (x + (3, 1)[k]) % 4, (zh + 4 - kz) % 4).at[pl.ds(k * 64, 64)]
        return rc(q, q, xc_s.at[kz, 2 + k], xc_r.at[kz, 2 + k], dev(x=(x + (1, 3)[k]) % 4))

    def x_relay_in(kz, k):
        q = piece(co, (x + 2) % 4, (zh + 4 - kz) % 4).at[pl.ds(k * 64, 64)]
        return rc(q, q, xc_s.at[kz, 2 + k], xc_r.at[kz, 2 + k], dev(co=1 - co))

    def c_out(kz, kx):
        q = piece(co, (x + 4 - kx) % 4, (zh + 4 - kz) % 4)
        return rc(q, q, cd_s.at[kz, kx], cd_r.at[kz, kx], dev(co=1 - co))

    def c_in(kz, kx):
        q = piece(1 - co, (x + 4 - kx) % 4, (zh + 4 - kz) % 4)
        return rc(q, q, cd_s.at[kz, kx], cd_r.at[kz, kx], dev(co=1 - co))

    def lc_part(p, h):
        return ac_ref.at[pl.ds(pl.multiple_of(p * NB + h * 64, 64), 64)]

    def lc_first(p, t):
        return rc(xb.at[pl.ds(t * 64, 64)], lc_part(p, t), lc_s.at[p, t], lc_r.at[p, 0], (t, col))

    def lc_out(p, k, src=None):
        q = lc_part(p, y)
        return rc(q if src is None else src, q, lc_s.at[p, 4 + k], lc_r.at[p, k], dev(y=(y + k) % 4))

    def lc_in(p, k):
        q = lc_part(p, (y + 4 - k) % 4)
        return rc(q, q, lc_s.at[p, 4 + k], lc_r.at[p, k], dev(co=1 - co))

    def lc_cross(p, src=None):
        q = lc_part(p, y)
        return rc(q if src is None else src, q, lc_s.at[p, 4], lc_r.at[p, 0], dev(zl=1))

    def column(z, what):
        def run(cp):
            cp.start() if what == "start" else cp.wait_send()

        @pl.when(zl == z)
        def _():
            for p in range(2):
                if what == "start":
                    if z == 1:
                        lc_in(p, 0).wait_recv()
                    else:

                        @pl.when(row != p)
                        def _():
                            lc_in(p, 0).wait_recv()

                for k in range(1, 4):
                    if z == 1:
                        run(lc_out(p, k))
                    else:

                        @pl.when((row != p) & ((y + k) % 4 != p))
                        def _():
                            run(lc_out(p, k))

                        @pl.when(row == p)
                        def _():
                            run(lc_out(p, k, xb.at[pl.ds(p * 64, 64)]))

    def column_cross(what):
        for p in range(2):
            for mine in (True, False):

                @pl.when((zl == 0) & ((row == p) if mine else (row != p)))
                def _():
                    cp = lc_cross(p, xb.at[pl.ds(p * 64, 64)] if mine else None)
                    cp.start() if what == "start" else cp.wait_send()

    def column_in():
        for p in range(2):

            @pl.when(row != p)
            def _():
                for k in range(1, 4):
                    lc_in(p, k).wait_recv()

    def diag_out(p):
        return rc(xb.at[:, pl.ds(0, NB)], d.at[pl.ds(p * NB, NB), pl.ds(NB, NB)], dg_s.at[0], dg_r.at[p], (0, 0))

    def diag_in(p):
        q = d.at[pl.ds(p * NB, NB), pl.ds(NB, NB)]
        return rc(q, q, dg_s.at[0], dg_r.at[p], (0, 1))

    def li_part(ref, c):
        i, j = CHUNKS[c]
        return ref.at[pl.ds(i * LEAF, LEAF), pl.ds(j * LEAF, LEAF)]

    def source_of(c):
        return li if CHUNKS[c][0] == CHUNKS[c][1] else d

    def li_out(c, ref, k, to):
        return rc(li_part(ref, c), li_part(lo_ref, c), li_s.at[c, k], li_r.at[c], to)

    def li_in(c):
        q = li_part(lo_ref, c)
        return rc(q, q, li_s.at[c, 0], li_r.at[c], dev(co=1 - co))

    def li_edge(c, ref, k, to, what, role):
        @pl.when(role)
        def _():
            cp = li_out(c, ref, k, to)
            cp.start() if what == "start" else cp.wait_send()

    def li_high(c, ref, what):
        mine = (row == 0) & (co == c % 2)
        for k in range(3):
            li_edge(c, ref, k, dev(x=(x + k + 1) % 4), what, mine & (zh == 0) & (x == 0))
        for k in range(2):
            li_edge(c, ref, 3 + k, dev(zh=(1, 3)[k]), what, mine & (zh == 0))
        li_edge(c, ref, 5, dev(zh=2), what, mine & (zh == 3))
        for k in (0, 2):
            li_edge(c, ref, 6 + k, dev(y=(y + k + 1) % 4), what, mine)

    def li_low(c, ref, what):
        mine = co == c % 2
        li_edge(c, ref, 7, dev(y=2), what, mine & (row == 3))
        li_edge(c, ref, 9, dev(zl=1), what, mine & (zl == 0) & (y != 0))
        li_edge(c, ref, 9, (4, ((zh + 3) % 4 * 4 + x) * 2 + co), what, mine & (row == 0))
        back = mine & jnp.logical_not((row == 0) & (col == 1))
        li_edge(c, ref, 10, dev(co=1 - co), what, back if c % 2 else mine)

    def li_early(chunks):
        @pl.when((row == 0) & jnp.logical_not(root))
        def _():
            for c in chunks:
                li_in(c).wait_recv()
                li_high(c, lo_ref, "start")
                li_low(c, lo_ref, "start")

    def li_late(chunks):
        @pl.when(row != 0)
        def _():
            for c in chunks:
                li_in(c).wait_recv()
                li_low(c, lo_ref, "start")

    def li_root(i):
        @pl.when(root)
        def _():
            if i == 1:
                for p in range(2):
                    diag_in(p).wait_recv()
                factor_second(d, li)
            if i:
                factor_block(i, 4, d, li)
            for c in STAGES[i]:
                ref = source_of(c)
                if c % 2:
                    li_out(c, ref, 11, dev(co=1)).start()
                else:
                    li_high(c, ref, "start")
                    li_low(c, ref, "start")
                pltpu.make_async_copy(li_part(ref, c), li_part(lo_ref, c), loc_sem.at[4 + c]).start()


    for p in range(2):

        @pl.when(row == p)
        def _():
            @pl.when(col == 1)
            def _():
                diag_out(p).start()

            @pl.when(col % 8 == row)
            def _():
                scatter_self().start()

            @pl.when(col % 8 != row)
            def _():
                scatter(0).start()

            for i in range(1, 4):
                scatter(i).start()
            for t in range(4):
                if t != p:
                    lc_first(p, t).start()
            pltpu.make_async_copy(xb, ac_ref.at[pl.ds(p * NB, NB)], loc_sem.at[1]).start()

    li_root(0)
    li_root(1)


    @pl.when(self_scatter)
    def _():
        scatter_self().wait()

    @pl.when(jnp.logical_not(self_scatter))
    def _():
        scatter_in().wait_recv()

    for k in (1, 3, 2):
        z_out(k).start()
    for k in range(2):
        x_out(0, k).start()
    c_out(0, 0).start()

    li_root(2)
    li_root(3)
    li_early(STAGES[0])

    def onward(kz):
        for k in range(2):
            x_out(kz, k).start()
        c_out(kz, 0).start()

    def from_x(kz):
        for k in range(2):
            x_in(kz, k).wait_recv()
            x_relay(kz, k).start()
            c_out(kz, (1, 3)[k]).start()

    def from_relay(kz):
        for k in range(2):
            x_relay_in(kz, k).wait_recv()
        c_out(kz, 2).start()

    column(0, "start")
    li_early(STAGES[1])
    z_in(1).wait_recv()
    onward(1)
    column_cross("start")
    for kz in (3, 2):
        z_in(kz).wait_recv()
        onward(kz)
    li_early(STAGES[2])
    from_x(0)
    li_early(STAGES[3])
    column(1, "start")
    from_x(1)
    li_late(STAGES[0] + STAGES[1])
    from_x(3)
    from_x(2)
    li_late(STAGES[2] + STAGES[3])
    for kz in (0, 1, 3, 2):
        from_relay(kz)
    column_in()

    for kz in range(4):
        for kx in range(4):
            c_in(kz, kx).wait_recv()
            c_out(kz, kx).wait_send()
        for k in range(2):
            x_out(kz, k).wait_send()
            x_relay(kz, k).wait_send()

    for k in range(1, 4):
        z_out(k).wait_send()

    for p in range(2):

        @pl.when(row == p)
        def _():
            @pl.when(col == 1)
            def _():
                diag_out(p).wait_send()

            for t in range(4):
                if t != p:
                    lc_first(p, t).wait_send()
            for q in range(1, 4):
                scatter(q).wait_send()

            @pl.when(col % 8 != row)
            def _():
                scatter(0).wait_send()

            pltpu.make_async_copy(xb, ac_ref.at[pl.ds(p * NB, NB)], loc_sem.at[1]).wait()

    column(0, "wait")
    column_cross("wait")
    column(1, "wait")

    for c in range(len(CHUNKS)):

        @pl.when((row == 0) & jnp.logical_not(root & (c % 2 == 1)))
        def _():
            li_high(c, lo_ref, "wait")

        li_low(c, lo_ref, "wait")

        @pl.when(root)
        def _():
            if c % 2:
                li_out(c, source_of(c), 11, dev(co=1)).wait_send()
            pltpu.make_async_copy(li_part(source_of(c), c), li_part(lo_ref, c), loc_sem.at[4 + c]).wait()


def gather(flat):
    any_spec = pl.BlockSpec(memory_space=pl.ANY)
    dma = pltpu.SemaphoreType.DMA
    return pl.pallas_call(
        gather_kernel,
        out_shape=[
            jax.ShapeDtypeStruct((2, 2048, NB), F32),
            jax.ShapeDtypeStruct((2 * NB, 2 * NB), F32),
            jax.ShapeDtypeStruct((2 * NB, 2 * NB), F32),
        ],
        in_specs=[pl.BlockSpec(memory_space=pltpu.HBM)],
        out_specs=[any_spec] * 3,
        scratch_shapes=[
            pltpu.VMEM((4 * NB, 128), F32),
            pltpu.VMEM((NB, 2 * NB), F32),
            pltpu.VMEM((2 * NB, NB), F32),
            pltpu.VMEM((2 * NB, 2 * NB), F32),
            pltpu.VMEM((2 * NB, 2 * NB), F32),
            dma, dma((14,)),
            dma((4,)), dma((1,)),
            dma((4,)), dma((4,)),
            dma((4, 4)), dma((4, 4)),
            dma((4, 4)), dma((4, 4)),
            dma((2, 11)), dma((2, 4)),
            dma((1,)), dma((2,)),
            dma((10, 12)), dma((10,)),
        ],
        compiler_params=pltpu.CompilerParams(collective_id=0, has_side_effects=True, vmem_limit_bytes=32 << 20),
        name="gather_panel",
    )(flat)


def halves(a):
    hi = a.astype(BF16)
    return hi, (a - hi.astype(F32)).astype(BF16)


def dot3(a, b, da=1, db=0):
    mm = lambda u, v: lax.dot_general(u, v, (((da,), (db,)), ((), ())), preferred_element_type=F32)
    return mm(a[0], b[0]) + (mm(a[0], b[1]) + mm(a[1], b[0]))


def update_kernel(x_ref, ar_ref, ac_ref, li_ref, o_ref, w, a, l_hi, l_lo):
    slot = pl.program_id(0)
    row = lax.axis_index("row")
    col = lax.axis_index("col")
    kk = 2 * NB

    @pl.when(slot == 0)
    def _():
        zero = jnp.zeros((LEAF, LEAF), BF16)
        for i in range(4):
            rows = pl.ds(i * LEAF, LEAF)
            v = li_ref[rows, rows]
            r = lax.broadcasted_iota(jnp.int32, v.shape, 0)
            c = lax.broadcasted_iota(jnp.int32, v.shape, 1)
            v = jnp.where(c <= r, v, 0.0)
            l_hi[rows, rows], l_lo[rows, rows] = halves(v)
            if i:
                left = pl.ds(0, i * LEAF)
                l_hi[rows, left], l_lo[rows, left] = halves(-dot_full(v, li_ref[rows, left]))
            for j in range(i + 1, 4):
                l_hi[rows, pl.ds(j * LEAF, LEAF)] = zero
                l_lo[rows, pl.ds(j * LEAF, LEAF)] = zero
        l = (l_hi[...], l_lo[...])
        ch, cl = halves(ac_ref[...])
        uh, ul = halves(dot3((l[0][:NB, :NB], l[1][:NB, :NB]), (ch[:NB], cl[:NB])))
        vh, vl = halves(dot3((l[0][NB:], l[1][NB:]), (ch, cl)))
        high = dot3((l[0][:NB, :NB], l[1][:NB, :NB]), (uh, ul), 0) + dot3((l[0][NB:, :NB], l[1][NB:, :NB]), (vh, vl), 0)
        low = dot3((l[0][NB:, NB:], l[1][NB:, NB:]), (vh, vl), 0)
        for p, part in enumerate((high, low)):
            hi, lo = halves(part)
            w[pl.ds(p * NB, NB), :] = hi
            w[pl.ds(kk + p * NB, NB), :] = lo
            w[pl.ds(2 * kk + p * NB, NB), :] = hi

    for p in range(2):
        hi, lo = halves(ar_ref[p])
        a[:, pl.ds(p * NB, NB)] = hi
        a[:, pl.ds(kk + p * NB, NB)] = hi
        a[:, pl.ds(2 * kk + p * NB, NB)] = lo
    grow = slot * 8 + row
    keep = grow >= 2

    def trail(half):
        upd = jnp.dot(a[...], w[:, pl.ds(half * NB, NB)], preferred_element_type=F32)
        for q in range(2):
            at = (0, pl.ds(2 * half + q, NB, stride=4), slice(None))
            o_ref[at] = jnp.where(keep, x_ref[at] - upd[:, q * LEAF : (q + 1) * LEAF], 0.0)

    trail(1)

    @pl.when((col >= 2) | ((col == 1) & (grow == 0)))
    def _():
        trail(0)

    def put(p, mask):
        n = (p + 1) * NB
        at = (pl.ds(p * NB, NB), pl.ds(0, n))
        v2 = dot3((a[:, pl.ds(0, n)], a[:, pl.ds(2 * kk, n)]), (l_hi[at], l_lo[at]), 1, 1)
        for q in range(2):
            v = v2[:, q * LEAF : (q + 1) * LEAF]
            r = lax.broadcasted_iota(jnp.int32, v.shape, 0)
            c = lax.broadcasted_iota(jnp.int32, v.shape, 1) + q * LEAF
            o_ref[0, pl.ds(q, NB, stride=4), :] = jnp.where((c <= r) | jnp.logical_not(mask), v, 0.0)

    @pl.when(col == 0)
    def _():
        put(0, grow == 0)

    @pl.when((col == 1) & (grow >= 1))
    def _():
        put(1, grow == 1)


def update(flat, ar, ac, li):
    whole = pl.BlockSpec((2 * NB, 2 * NB), lambda s: (0, 0))
    slab = pl.BlockSpec((1, 4 * NB, 128), lambda s: (s, 0, 0))
    return pl.pallas_call(
        update_kernel,
        grid=(8,),
        out_shape=jax.ShapeDtypeStruct(flat.shape, F32),
        in_specs=[slab, pl.BlockSpec((2, NB, NB), lambda s: (0, s, 0)), whole, whole],
        out_specs=slab,
        scratch_shapes=[
            pltpu.VMEM((6 * NB, 2 * NB), BF16),
            pltpu.VMEM((NB, 6 * NB), BF16),
            pltpu.VMEM((2 * NB, 2 * NB), BF16),
            pltpu.VMEM((2 * NB, 2 * NB), BF16),
        ],
        compiler_params=pltpu.CompilerParams(vmem_limit_bytes=32 << 20),
        name="update_trailing",
    )(flat, ar, ac, li)


def body(matrix):
    flat = matrix.reshape(8 * 4 * NB, 128)
    ar, ac, li = gather(flat)
    return update(flat.reshape(8, 4 * NB, 128), ar, ac, li).reshape(matrix.shape)


def solution(mesh):
    spec = P(None, "row", None, None, "col", None)
    return jax.shard_map(body, mesh=mesh, in_specs=(spec,), out_specs=spec, check_vma=False)
```
